32 devices in a mesh: front: 2 (over y), row: 4 (over x, core), col: 4 (over z).
Axes of the slice: x: 2, y: 2, z: 4, core: 2. Of those that a mesh axis runs over, the one named last changes fastest.
Arguments:
- kids: bfloat16 [2, 2, 3072, 3072], P('front', None, 'row'), as said below
- maps: int32 [2, 2, 72, 24], P('front'), may hold values from 0 to 1, as said below
- mask: int32 [2, 72, 4], P('front'), may hold values 0 or 1
- diag: float32 [2, 9216], P('front', 'row'), may hold values from 1 to 2
Outputs:
- front: float32 [2, 9216, 512], P('front', 'row', 'col')
The draws below stay inside these ranges and needn't reach their ends.
Inputs may be any that keep to these rules, and one draw needn't show every extreme that they name: Each kids[f, k] is symmetric. Each maps[f, k] has a single 1 in every column and at most one 1 in every row; all other entries are 0.
All inputs are finite; a program needn't handle non-finite values. No bound on the sum of `mask` on one device may be relied on, other than what follows from the above.
Results may differ from the reference program's by a relative error of at most 0.0003.
Values may be sent and summed in bfloat16 or wider, within the bound.
No kernel may reach another device: no remote copies, remote signals or barrier semaphores. Data moves between devices by JAX's collectives and lax.ppermute only.
A program may use at most 128 MiB of HBM per device.

```python
import jax
import jax.numpy as jnp
from jax import lax

BLOCK = 128
F = 9216
G = 3072
PW = 128
NPANEL = 2
FRONTS = 2
WC = 512
FB = 72
GB = 24
WB = 4


def draw_kids(key, part):
    key = jax.random.fold_in(key, 3)
    full_shape = (FRONTS, 2, G, G)
    entry_key, weight_key = jax.random.split(key)
    entries = jnp.clip(jax.random.normal(entry_key, full_shape, jnp.float32), -6.0, 6.0)
    weights = jax.random.uniform(weight_key, (FRONTS, 2, G), jnp.float32, 0.5, 1.5)
    common = 0.2 * weights[..., :, None] * weights[..., None, :]
    jitter = (entries + jnp.swapaxes(entries, -1, -2)) * 0.014142136
    return (common + jitter).astype(jnp.bfloat16)


def one_map(key):
    chosen = jax.random.permutation(key, FB)[:GB]
    return (jnp.arange(FB)[:, None] == chosen[None, :]).astype(jnp.int32)


def draw_maps(key, part):
    key = jax.random.fold_in(key, 7)
    keys = jax.random.split(key, FRONTS * 2)
    tables = jax.vmap(one_map)(keys)
    return tables.reshape(FRONTS, 2, FB, GB)


def set_ends(array, own_key, least, high):
    longest = array.shape.index(max(array.shape))
    spots = []
    for shift in (0, 1):
        where = [jax.random.randint(jax.random.fold_in(own_key, axis), (), 0, length) for axis, length in enumerate(array.shape)]
        where[longest] = (where[longest] + shift) % array.shape[longest]
        spots.append(tuple(where))
    return array.at[spots[0]].set(least).at[spots[1]].set(high)


def shard_levels(stream_key, extent, cuts, low, largest):
    gain, own = 1.0, jax.random.fold_in(stream_key, 6)
    for axis_at, blocks in cuts:
        draws = jnp.exp(jax.random.uniform(jax.random.fold_in(own, axis_at), (blocks,), jnp.float32, low / len(cuts), largest / len(cuts)))
        gain = gain * jnp.repeat(draws, extent[axis_at] // blocks).reshape([-1 if axis == axis_at else 1 for axis in range(len(extent))])
    return gain


def setup_inputs(seed: int = 0) -> dict:
    streams_of = jax.random.split(jax.random.key(seed), 5)
    return {
        "kids": draw_kids(jax.random.fold_in(streams_of[4], 71), 0),
        "maps": draw_maps(jax.random.fold_in(streams_of[4], 71), 0),
        "mask": set_ends((jax.random.randint(streams_of[2], (FRONTS, FB, WB), 0, 2) < 1).astype(jnp.int32), jax.random.fold_in(streams_of[2], 1), 0, 1),
        "diag": jnp.clip(1.0 + 1.0 * jax.random.uniform(streams_of[3], (FRONTS, F), jnp.float32) ** shard_levels(streams_of[3], (FRONTS, F), ((0, 2), (1, 4)), -0.2, 0.2), 1.0, 2.0),
    }


def extend(child, row_map):
    rows_map = row_map.astype(jnp.float32)
    cols_map = rows_map[:WB]
    shaped = child.astype(jnp.float32).reshape(GB, BLOCK, GB, BLOCK)
    picked = jnp.einsum('wk,jakb->jawb', cols_map, shaped, precision=lax.Precision.HIGHEST)
    placed = jnp.einsum('pj,jawb->pawb', rows_map, picked, precision=lax.Precision.HIGHEST)
    return placed.reshape(F, WC)

def one_front(index, kids, maps, mask, diag):
    nearby = (index + 1) % FRONTS
    matrix = extend(kids[index, 0], maps[index, 0]) + extend(kids[nearby, 1], maps[nearby, 1])
    row_ids = jnp.arange(F)[:, None]
    col_ids = jnp.arange(WC)[None, :]
    matrix = matrix + jnp.where(row_ids == col_ids, diag[index][:, None], jnp.float32(0.0))
    expanded = jnp.repeat(jnp.repeat(mask[index].astype(jnp.float32), BLOCK, 0), BLOCK, 1)
    update_mask = jnp.where(col_ids < NPANEL * PW, jnp.float32(1.0), expanded)
    for panel_index in range(NPANEL):
        lower = panel_index * PW
        upper = lower + PW
        column_slab = matrix[:, lower:upper]
        factor = jnp.linalg.cholesky(column_slab[lower:upper])
        solved = lax.linalg.triangular_solve(factor, column_slab, left_side=False, lower=True, transpose_a=True)
        padded = jnp.pad(factor, ((lower, F - upper), (0, 0)))
        inside = (row_ids >= lower) & (row_ids < upper)
        panel_rows = jnp.where(inside, padded, jnp.where(row_ids >= upper, solved, jnp.float32(0.0)))
        product = jnp.dot(panel_rows, panel_rows[:WC].T, precision=lax.Precision.HIGHEST)
        matrix = matrix - jnp.where(col_ids >= upper, update_mask, jnp.float32(0.0)) * product
        matrix = matrix.at[:, lower:upper].set(panel_rows)
    return matrix

def reference(kids, maps, mask, diag):
    return jnp.stack([one_front(index, kids, maps, mask, diag) for index in range(FRONTS)])
```

```python
import functools

import jax
import jax.numpy as jnp
from jax import lax
from jax.experimental import pallas as pl
from jax.experimental.pallas import tpu as pltpu
from jax.sharding import PartitionSpec as P

BLOCK = 128
PW = 128
NPANEL = 2
F32 = jnp.float32
BF16 = jnp.bfloat16
HIGHEST = lax.Precision.HIGHEST
VMEM_LIMIT = 40 * 1024 * 1024


def params():
    return pltpu.CompilerParams(vmem_limit_bytes=VMEM_LIMIT)


def child_block(maps, child, row):
    index, found = jnp.int32(0), jnp.int32(0)
    for j in range(maps.shape[3]):
        value = maps[0, child, row, j]
        index = index + value * j
        found = found + value
    return index, found


def window_kernel(maps, diag, kids, own, far, sems):
    me = lax.axis_index("row")
    local = kids.shape[2] // BLOCK
    copies = []
    for child, out in ((0, own), (1, far)):
        found = [child_block(maps, child, w) for w in range(NPANEL)]
        for at, (w, p) in enumerate(((0, 0), (1, 0), (1, 1))):
            row, row_ok = found[w]
            col, col_ok = found[p]
            offset = row - me * local
            here = (row_ok > 0) & (col_ok > 0) & (offset >= 0) & (offset < local)
            target = out.at[pl.ds(at * BLOCK, BLOCK)]
            copy = pltpu.make_async_copy(
                kids.at[
                    0,
                    child,
                    pl.ds(pl.multiple_of(offset * BLOCK, BLOCK), BLOCK),
                    pl.ds(pl.multiple_of(col * BLOCK, BLOCK), BLOCK),
                ],
                target,
                sems.at[child, at],
            )
            copies.append((here, copy, target))
    for here, copy, target in copies:

        @pl.when(here)
        def _():
            copy.start()

        @pl.when(jnp.logical_not(here))
        def _():
            target[...] = jnp.zeros_like(target)

    line = lax.broadcasted_iota(jnp.int32, (16, BLOCK), 0)
    pieces = jnp.zeros((16, BLOCK), F32)
    for p in range(NPANEL):
        rest = jnp.broadcast_to(diag[0:1, p * PW : (p + 1) * PW], (16, BLOCK))
        for at in range(3):
            part = rest.astype(BF16).astype(F32)
            pieces = jnp.where(line == 3 * p + at, part, pieces)
            rest = rest - part
    own[3 * BLOCK :, :] = jnp.where(me == 0, pieces, 0.0).astype(BF16)
    for here, copy, target in copies:

        @pl.when(here)
        def _():
            copy.wait()


def bands_kernel(maps, kids, own, far, sems):
    col_index = lax.axis_index("col")
    copies = []
    for child, out in ((0, own), (1, far)):
        for at, row in enumerate((0, 1, col_index)):
            col, ok = child_block(maps, child, row)
            target = out.at[:, pl.ds(at * BLOCK, BLOCK)]
            copy = pltpu.make_async_copy(
                kids.at[0, child, :, pl.ds(pl.multiple_of(col * BLOCK, BLOCK), BLOCK)],
                target,
                sems.at[child, at],
            )
            copies.append((ok > 0, copy, target))
    for here, copy, target in copies:

        @pl.when(here)
        def _():
            copy.start()

        @pl.when(jnp.logical_not(here))
        def _():
            target[...] = jnp.zeros_like(target)

    for here, copy, target in copies:

        @pl.when(here)
        def _():
            copy.wait()


def inverse_factor(tiles):
    tiles = list(tiles)
    count = len(tiles)
    lane = lax.broadcasted_iota(jnp.int32, (8, BLOCK), 1)
    line = lax.broadcasted_iota(jnp.int32, (8, BLOCK), 0)
    wide = lambda x: jnp.broadcast_to(x, (8, BLOCK))
    result = []
    for b in range(count):
        low = 8 * b
        tile = tiles[b]
        columns = [wide(tile[:, low + j : low + j + 1]) for j in range(8)]
        d = [[wide(columns[j][i : i + 1, :]) if i >= j else None for j in range(8)] for i in range(8)]
        inside = (lane >= low) & (lane < low + 8)
        rows = [
            jnp.where(inside, (lane == low + i).astype(F32), wide(tile[i : i + 1, :]))
            for i in range(8)
        ]
        scale = []
        for j in range(8):
            scale.append(lax.rsqrt(d[j][j]))
            for i in range(j + 1, 8):
                d[i][j] = d[i][j] * scale[j]
            for k in range(j + 1, 8):
                for i in range(k, 8):
                    d[i][k] = d[i][k] - d[i][j] * d[k][j]
            rows[j] = rows[j] * scale[j]
            for i in range(j + 1, 8):
                rows[i] = rows[i] - d[i][j] * rows[j]
        merged = rows[0]
        for j in range(1, 8):
            merged = jnp.where(line == j, rows[j], merged)
        result.append(jnp.where(lane < low + 8, merged, 0.0))
        for t in range(b + 1, count):
            tile = tiles[t]
            columns = [wide(tile[:, low + j : low + j + 1]) for j in range(8)]
            tile = jnp.where(inside, 0.0, tile)
            for j in range(8):
                for m in range(j):
                    columns[j] = columns[j] - columns[m] * d[j][m]
                columns[j] = columns[j] * scale[j]
                tile = tile - columns[j] * rows[j]
            tiles[t] = tile
    return result


def dot(a, b, lhs=1, rhs=0):
    return lax.dot_general(
        a, b, (((lhs,), (rhs,)), ((), ())), precision=HIGHEST, preferred_element_type=F32
    )


def factor_kernel(n_own, *refs):
    own, far, out = refs[:n_own], refs[n_own:-1], refs[-1]

    def total(at):
        value = None
        for ref in own + far:
            block = ref[at * BLOCK : (at + 1) * BLOCK, :].astype(F32)
            value = block if value is None else value + block
        return value

    pieces = None
    for ref in own:
        part = ref[3 * BLOCK :, :].astype(F32)
        pieces = part if pieces is None else pieces + part
    eye = lax.broadcasted_iota(jnp.int32, (BLOCK, BLOCK), 0) == lax.broadcasted_iota(
        jnp.int32, (BLOCK, BLOCK), 1
    )

    def diagonal(p):
        line = pieces[3 * p : 3 * p + 1] + pieces[3 * p + 1 : 3 * p + 2]
        line = line + pieces[3 * p + 2 : 3 * p + 3]
        return jnp.where(eye, jnp.broadcast_to(line, (BLOCK, BLOCK)), 0.0)

    def invert(block):
        return jnp.concatenate(
            inverse_factor([block[8 * t : 8 * t + 8, :] for t in range(BLOCK // 8)]), axis=0
        )

    first = invert(total(0) + diagonal(0))
    cross = dot(total(1), first, 1, 1)
    second = invert(total(2) + diagonal(1) - dot(cross, cross, 1, 1))
    out[0:BLOCK, 0:BLOCK] = first
    out[0:BLOCK, BLOCK:] = jnp.zeros((BLOCK, BLOCK), F32)
    out[BLOCK:, 0:BLOCK] = -dot(second, dot(cross, first))
    out[BLOCK:, BLOCK:] = second


def front_kernel(owners, n_row, row_blocks, tables, mask, diag, inverse, *refs):
    count = len(owners(0))
    own, far = refs[:count], refs[count : 2 * count]
    out, buffer, sems = refs[2 * count :]
    me = lax.axis_index("row")
    col_index = lax.axis_index("col")
    rows_here = own[0].shape[0]
    zero_block = n_row * rows_here // BLOCK
    copies = []
    for child, group in ((0, own), (1, far)):
        for at, (owner, ref) in enumerate(zip(owners(me), group)):
            copy = pltpu.make_async_copy(
                ref,
                buffer.at[child, pl.ds(pl.multiple_of(owner * rows_here, BLOCK), rows_here)],
                sems.at[child, at],
            )
            copy.start()
            copies.append(copy)
        buffer[child, zero_block * BLOCK :, :] = jnp.zeros((BLOCK, buffer.shape[2]), BF16)
    for copy in copies:
        copy.wait()

    def block(child, index, start, width):
        return buffer[child, pl.ds(pl.multiple_of(index * BLOCK, BLOCK), BLOCK), start : start + width]

    wide = NPANEL * PW
    lower = inverse[...]
    mirrored = block(0, tables[0, col_index], 0, wide).astype(F32) + block(
        1, tables[1, col_index], 0, wide
    ).astype(F32)
    row_id = lax.broadcasted_iota(jnp.int32, (wide, PW), 0)
    col_id = lax.broadcasted_iota(jnp.int32, (wide, PW), 1)
    picked = -(row_id == col_id + col_index * PW).astype(F32)
    solved = jnp.where(col_index < NPANEL, picked, dot(lower, mirrored, 1, 1))
    weight = dot(lower, solved, 0, 0)
    high = weight.astype(BF16)
    low = (weight - high.astype(F32)).astype(BF16)
    both = jnp.concatenate([high, low], axis=1)
    both = jnp.concatenate([both, both], axis=0)
    is_panel = col_index < NPANEL
    for p in range(row_blocks):
        at = me * row_blocks + p
        first, second = tables[0, at], tables[1, at]
        left = jnp.concatenate([block(0, first, 0, wide), block(1, second, 0, wide)], axis=1)
        product = jnp.dot(left, both, preferred_element_type=F32)
        product = product[:, :PW] + product[:, PW:]
        base = block(0, first, wide, PW).astype(F32) + block(1, second, wide, PW).astype(F32)
        keep = jnp.where(is_panel | (mask[0, at, col_index] > 0), 1.0, 0.0)
        out[0, p * BLOCK : (p + 1) * BLOCK, :] = jnp.where(is_panel, 0.0, base) - keep * product

    eye = lax.broadcasted_iota(jnp.int32, (BLOCK, BLOCK), 0) == lax.broadcasted_iota(
        jnp.int32, (BLOCK, BLOCK), 1
    )

    def diagonal(p):
        return jnp.where(
            eye, jnp.broadcast_to(diag[0:1, p * BLOCK : (p + 1) * BLOCK], (BLOCK, BLOCK)), 0.0
        )

    for p in range(NPANEL):

        @pl.when(me == 0)
        def _():
            keep = jnp.where(is_panel | (mask[0, p, col_index] > 0), 1.0, 0.0)
            column = jnp.sum(diagonal(p), axis=1, keepdims=True)
            value = out[0, p * BLOCK : (p + 1) * BLOCK, :]
            value = value - keep * column * weight[p * BLOCK : (p + 1) * BLOCK, :]
            row = lax.broadcasted_iota(jnp.int32, (BLOCK, BLOCK), 0) + p * BLOCK
            col = lax.broadcasted_iota(jnp.int32, (BLOCK, BLOCK), 1) + col_index * PW
            out[0, p * BLOCK : (p + 1) * BLOCK, :] = jnp.where(is_panel & (row < col), 0.0, value)

    for p in range(row_blocks):

        @pl.when(jnp.logical_not(is_panel) & (me * row_blocks + p == col_index))
        def _():
            out[0, p * BLOCK : (p + 1) * BLOCK, :] += diagonal(p)


def body(kids, maps, mask, diag):
    fronts, n_row = lax.axis_size("front"), lax.axis_size("row")
    chips = n_row // 2
    rows_dev = diag.shape[1]
    row_blocks = rows_dev // BLOCK
    rows_here = kids.shape[2]
    vmem, smem = pl.BlockSpec(memory_space=pltpu.VMEM), pl.BlockSpec(memory_space=pltpu.SMEM)
    anywhere = pl.BlockSpec(memory_space=pl.ANY)

    def along(x, by):
        return lax.ppermute(x, "row", [(i, (i + 2 * by) % n_row) for i in range(n_row)])

    def partner(x):
        return lax.ppermute(x, "row", [(i, i ^ 1) for i in range(n_row)])

    def parent(x, by):
        pairs = []
        for f in range(fronts):
            for i in range(n_row):
                pairs.append((f * n_row + i, (f - 1) % fronts * n_row + (i + 2 * by) % n_row))
        return lax.ppermute(x, ("front", "row"), pairs)

    own_window, far_window = pl.pallas_call(
        window_kernel,
        out_shape=[
            jax.ShapeDtypeStruct((3 * BLOCK + 16, BLOCK), BF16),
            jax.ShapeDtypeStruct((3 * BLOCK, BLOCK), BF16),
        ],
        in_specs=[smem, vmem, anywhere],
        out_specs=[vmem, vmem],
        scratch_shapes=[pltpu.SemaphoreType.DMA((2, 3))],
        compiler_params=params(),
        name="window_blocks",
    )(maps, diag, kids)
    own_parts = [own_window] + [along(own_window, s) for s in range(1, chips)]
    far_parts = [parent(far_window, s) for s in range(chips)]
    own_parts = own_parts + [partner(x) for x in own_parts]
    far_parts = far_parts + [partner(x) for x in far_parts]

    own_bands, far_bands = pl.pallas_call(
        bands_kernel,
        out_shape=[jax.ShapeDtypeStruct((rows_here, 3 * BLOCK), BF16)] * 2,
        in_specs=[smem, anywhere],
        out_specs=[vmem, vmem],
        scratch_shapes=[pltpu.SemaphoreType.DMA((2, 3))],
        compiler_params=params(),
        name="bands",
    )(maps, kids)
    far_bands = parent(far_bands, 0)
    own_all = [own_bands] + [along(own_bands, s) for s in range(1, chips)]
    far_all = [far_bands] + [along(far_bands, s) for s in range(1, chips)]
    own_all = own_all + [partner(x) for x in own_all]
    far_all = far_all + [partner(x) for x in far_all]

    def owners(me):
        here = [(me + n_row - 2 * s) % n_row for s in range(chips)]
        other = me + 1 - 2 * (me % 2)
        return here + [(other + n_row - 2 * s) % n_row for s in range(chips)]

    inverse = pl.pallas_call(
        functools.partial(factor_kernel, len(own_parts)),
        out_shape=jax.ShapeDtypeStruct((NPANEL * PW, NPANEL * PW), F32),
        compiler_params=params(),
        name="factor",
    )(*own_parts, *far_parts)

    count = maps.shape[3]
    found = jnp.sum(maps[0], axis=2)
    table = jnp.sum(maps[0] * jnp.arange(count), axis=2) + (1 - found) * count
    tables = jnp.stack([table[0], parent(table[1], 0)])

    return pl.pallas_call(
        functools.partial(front_kernel, owners, n_row, row_blocks),
        out_shape=jax.ShapeDtypeStruct((1, rows_dev, PW), F32),
        in_specs=[smem, smem, vmem, vmem] + [anywhere] * (2 * len(own_all)),
        out_specs=vmem,
        scratch_shapes=[
            pltpu.VMEM((2, n_row * rows_here + BLOCK, 3 * BLOCK), BF16),
            pltpu.SemaphoreType.DMA((2, len(own_all))),
        ],
        compiler_params=params(),
        name="front",
    )(tables, mask, diag, inverse, *own_all, *far_all)


def solution(mesh):
    in_specs = (
        P("front", None, "row", None),
        P("front", None, None, None),
        P("front", None, None),
        P("front", "row"),
    )
    out_specs = P("front", "row", "col")
    return jax.shard_map(body, mesh=mesh, in_specs=in_specs, out_specs=out_specs, check_vma=False)
```

```python
import functools

import jax
import jax.numpy as jnp
from jax import lax
from jax.experimental import pallas as pl
from jax.experimental.pallas import tpu as pltpu
from jax.sharding import PartitionSpec as P

BLOCK = 128
PW = 128
NPANEL = 2
F32 = jnp.float32
BF16 = jnp.bfloat16
HIGHEST = lax.Precision.HIGHEST
MIB = 1024 * 1024


def params(mib=40):
    return pltpu.CompilerParams(vmem_limit_bytes=mib * MIB)


def select_kernel(maps, diag, kids, tables, *refs):
    own_side, own_rest, far_window, far_side, far_pair, far_column, sems = refs
    lines = far_window.shape[0]
    me, col_index = lax.axis_index("row"), lax.axis_index("col")
    rows = kids.shape[2]
    local = rows // BLOCK
    none = kids.shape[3] // BLOCK
    places = maps.shape[3]
    child_id = lax.broadcasted_iota(jnp.int32, (none, places), 0)
    place_id = lax.broadcasted_iota(jnp.int32, (1, places), 1)
    found = []
    for child in range(2):
        ones = maps[0, child].astype(F32)
        line = jnp.sum(ones * (child_id - none).astype(F32), axis=0, keepdims=True) + none
        tables[child : child + 1, :] = line.astype(jnp.int32)
        found.append(
            [
                jnp.sum(jnp.where(place_id == w, line, 0.0)).astype(jnp.int32)
                for w in (0, 1, col_index)
            ]
        )
        if child == 1:
            line = jnp.broadcast_to(line, (16, places)).astype(BF16)
            far_side[3 * BLOCK : lines, 0:places] = line
            far_window[3 * BLOCK :, 0:places] = line
    copies = []

    def add(here, source, target):
        copy = pltpu.make_async_copy(source, target, sems.at[len(copies)])
        copies.append((here, copy))

        @pl.when(here)
        def _():
            copy.start()

        @pl.when(jnp.logical_not(here))
        def _():
            target[...] = jnp.zeros_like(target)

    def columns(start, size, child, col):
        return kids.at[0, child, pl.ds(start, size), pl.ds(pl.multiple_of(col * BLOCK, BLOCK), BLOCK)]

    for child, out in ((1, far_window), (0, own_side), (1, far_side)):
        for at, (w, p) in enumerate(((0, 0), (1, 0), (1, 1))):
            row, col = found[child][w], found[child][p]
            offset = row - me * local
            here = (row < none) & (col < none) & (offset >= 0) & (offset < local)
            start = pl.multiple_of(offset * BLOCK, BLOCK)
            add(here, columns(start, BLOCK, child, col), out.at[pl.ds(at * BLOCK, BLOCK)])
    half = rows // 2
    here, other = (
        pl.multiple_of(side * half, half) for side in (col_index % 2, 1 - col_index % 2)
    )
    side = [(0, here, half), (1, here, half)]
    rest = [(0, other, half), (1, other, half)]
    column = [(2, 0, rows)]
    for child, out, at, parts in (
        (0, own_side, lines, side + column),
        (1, far_side, lines, side + column),
        (1, far_pair, 0, side + rest),
        (1, far_column, 0, column),
        (0, own_rest, 0, rest),
    ):
        for p, start, size in parts:
            col = found[child][p]
            add(col < none, columns(start, size, child, col), out.at[pl.ds(at, size)])
            at += size

    line = lax.broadcasted_iota(jnp.int32, (16, BLOCK), 0)
    pieces = jnp.zeros((16, BLOCK), F32)
    for p in range(NPANEL):
        rest = jnp.broadcast_to(diag[0:1, p * PW : (p + 1) * PW], (16, BLOCK))
        for at in range(3):
            part = rest.astype(BF16).astype(F32)
            pieces = jnp.where(line == 3 * p + at, part, pieces)
            rest = rest - part
    own_side[3 * BLOCK : lines, :] = jnp.where(me == 0, pieces, 0.0).astype(BF16)
    for here, copy in copies:

        @pl.when(here)
        def _():
            copy.wait()


def cost(microseconds):
    return pl.CostEstimate(flops=microseconds * 10**9, bytes_accessed=0, transcendentals=0)


def inverse_factor(tiles):
    tiles = list(tiles)
    count = len(tiles)
    lane = lax.broadcasted_iota(jnp.int32, (8, BLOCK), 1)
    line = lax.broadcasted_iota(jnp.int32, (8, BLOCK), 0)
    wide = lambda x: jnp.broadcast_to(x, (8, BLOCK))
    result = []
    for b in range(count):
        low = 8 * b
        tile = tiles[b]
        columns = [wide(tile[:, low + j : low + j + 1]) for j in range(8)]
        d = [[wide(columns[j][i : i + 1, :]) if i >= j else None for j in range(8)] for i in range(8)]
        inside = (lane >= low) & (lane < low + 8)
        rows = [
            jnp.where(inside, (lane == low + i).astype(F32), wide(tile[i : i + 1, :]))
            for i in range(8)
        ]
        scale = []
        for j in range(8):
            scale.append(lax.rsqrt(d[j][j]))
            for i in range(j + 1, 8):
                d[i][j] = d[i][j] * scale[j]
            for k in range(j + 1, 8):
                for i in range(k, 8):
                    d[i][k] = d[i][k] - d[i][j] * d[k][j]
            rows[j] = rows[j] * scale[j]
            for i in range(j + 1, 8):
                rows[i] = rows[i] - d[i][j] * rows[j]
        merged = rows[0]
        for j in range(1, 8):
            merged = jnp.where(line == j, rows[j], merged)
        result.append(jnp.where(lane < low + 8, merged, 0.0))
        for t in range(b + 1, count):
            tile = tiles[t]
            columns = [wide(tile[:, low + j : low + j + 1]) for j in range(8)]
            tile = jnp.where(inside, 0.0, tile)
            for j in range(8):
                for m in range(j):
                    columns[j] = columns[j] - columns[m] * d[j][m]
                columns[j] = columns[j] * scale[j]
                tile = tile - columns[j] * rows[j]
            tiles[t] = tile
    return result


def dot(a, b, lhs=1, rhs=0):
    return lax.dot_general(
        a, b, (((lhs,), (rhs,)), ((), ())), precision=HIGHEST, preferred_element_type=F32
    )


def factor_kernel(n_own, *refs):
    own, far, out = refs[:n_own], refs[n_own:-1], refs[-1]

    def total(at):
        value = None
        for ref in own + far:
            block = ref[at * BLOCK : (at + 1) * BLOCK, :].astype(F32)
            value = block if value is None else value + block
        return value

    pieces = None
    for ref in own:
        part = ref[3 * BLOCK : 3 * BLOCK + 16, :].astype(F32)
        pieces = part if pieces is None else pieces + part
    eye = lax.broadcasted_iota(jnp.int32, (BLOCK, BLOCK), 0) == lax.broadcasted_iota(
        jnp.int32, (BLOCK, BLOCK), 1
    )

    def diagonal(p):
        line = pieces[3 * p : 3 * p + 1] + pieces[3 * p + 1 : 3 * p + 2]
        line = line + pieces[3 * p + 2 : 3 * p + 3]
        return jnp.where(eye, jnp.broadcast_to(line, (BLOCK, BLOCK)), 0.0)

    def invert(block):
        return jnp.concatenate(
            inverse_factor([block[8 * t : 8 * t + 8, :] for t in range(BLOCK // 8)]), axis=0
        )

    first = invert(total(0) + diagonal(0))
    cross = dot(total(1), first, 1, 1)
    second = invert(total(2) + diagonal(1) - dot(cross, cross, 1, 1))
    out[0:BLOCK, 0:BLOCK] = first
    out[0:BLOCK, BLOCK:] = jnp.zeros((BLOCK, BLOCK), F32)
    out[BLOCK:, 0:BLOCK] = -dot(second, dot(cross, first))
    out[BLOCK:, BLOCK:] = second


def product_kernel(layout, n_row, lines, tables, inverse, *refs):
    sources = list(refs[:-2])
    weight, product = refs[-2:]
    me, col_index = lax.axis_index("row"), lax.axis_index("col")
    rows = (product.shape[1] - BLOCK) // n_row
    half = rows // 2
    wide = NPANEL * PW
    parts = []
    for child, owner, whole in layout:
        first = sources.pop(0)
        second = first if whole else sources.pop(0)
        parts.append((child, owner(me), first, 0 if whole else lines, col_index % 2))
        parts.append((child, owner(me), second, rows if whole else 0, 1 - col_index % 2))

    mirrored = jnp.zeros((BLOCK, wide), F32)
    for child, owner, ref, at, side in parts:
        index = tables[child, col_index] * BLOCK
        for step in range(0, BLOCK, BLOCK // 2):
            place = index + step - owner * rows - side * half
            inside = (place >= 0) & (place < half)
            place = pl.multiple_of(jnp.where(inside, place, 0), BLOCK // 2)
            lines = [ref[pl.ds(at + p * half + place, BLOCK // 2), :] for p in range(NPANEL)]
            lines = jnp.where(inside, jnp.concatenate(lines, axis=1).astype(F32), 0.0)
            empty = jnp.zeros_like(lines)
            lines = [lines, empty] if step == 0 else [empty, lines]
            mirrored = mirrored + jnp.concatenate(lines, axis=0)

    lower = inverse[...]
    row_id = lax.broadcasted_iota(jnp.int32, (wide, PW), 0)
    col_id = lax.broadcasted_iota(jnp.int32, (wide, PW), 1)
    picked = -(row_id == col_id + col_index * PW).astype(F32)
    solved = jnp.where(col_index < NPANEL, picked, dot(lower, mirrored, 1, 1))
    weight[...] = dot(lower, solved, 0, 0)
    high = weight[...].astype(BF16)
    low = (weight[...] - high.astype(F32)).astype(BF16)
    both = jnp.concatenate([high, low], axis=1)
    for child, owner, ref, at, side in parts:
        left = jnp.concatenate([ref[at + p * half : at + (p + 1) * half, :] for p in range(NPANEL)], axis=1)
        value = jnp.dot(left, both, preferred_element_type=F32)
        start = pl.multiple_of(owner * rows + side * half, half)
        product[child, pl.ds(start, half), :] = value[:, :PW] + value[:, PW:]
    for child in range(2):
        product[child, n_row * rows :, :] = jnp.zeros((BLOCK, PW), F32)


def front_kernel(layout, n_row, row_blocks, tables, mask, diag, weight, product, *refs):
    sources = refs[: len(layout)]
    out, buffer = refs[len(layout) :]
    me, col_index = lax.axis_index("row"), lax.axis_index("col")
    rows = (product.shape[1] - BLOCK) // n_row
    is_panel = col_index < NPANEL
    for (child, owner, at), ref in zip(layout, sources):
        start = pl.multiple_of(owner(me) * rows, rows)
        buffer[child, pl.ds(start, rows), :] = ref[at : at + rows, :]
    for child in range(2):
        buffer[child, n_row * rows :, :] = jnp.zeros((BLOCK, PW), BF16)
    for p in range(row_blocks):
        at = me * row_blocks + p
        first, second = (
            pl.ds(pl.multiple_of(tables[child, at] * BLOCK, BLOCK), BLOCK) for child in range(2)
        )
        base = buffer[0, first, :].astype(F32) + buffer[1, second, :].astype(F32)
        keep = jnp.where(is_panel | (mask[0, col_index, at] > 0), 1.0, 0.0)
        value = jnp.where(is_panel, 0.0, base) - keep * (product[0, first, :] + product[1, second, :])
        out[0, p * BLOCK : (p + 1) * BLOCK, :] = value

    row_id = lax.broadcasted_iota(jnp.int32, (BLOCK, BLOCK), 0)
    col_id = lax.broadcasted_iota(jnp.int32, (BLOCK, BLOCK), 1)

    def diagonal(p):
        line = jnp.broadcast_to(diag[0:1, p * BLOCK : (p + 1) * BLOCK], (BLOCK, BLOCK))
        return jnp.where(row_id == col_id, line, 0.0)

    for p in range(NPANEL):

        @pl.when(me == 0)
        def _():
            keep = jnp.where(is_panel | (mask[0, col_index, p] > 0), 1.0, 0.0)
            column = jnp.sum(diagonal(p), axis=1, keepdims=True)
            value = out[0, p * BLOCK : (p + 1) * BLOCK, :]
            value = value - keep * column * weight[p * BLOCK : (p + 1) * BLOCK, :]
            above = row_id + p * BLOCK < col_id + col_index * PW
            out[0, p * BLOCK : (p + 1) * BLOCK, :] = jnp.where(is_panel & above, 0.0, value)

    for p in range(row_blocks):

        @pl.when(jnp.logical_not(is_panel) & (me * row_blocks + p == col_index))
        def _():
            out[0, p * BLOCK : (p + 1) * BLOCK, :] += diagonal(p)


def body(kids, maps, mask, diag):
    fronts, n_row, n_col = (lax.axis_size(name) for name in ("front", "row", "col"))
    chips = n_row // 2
    rows_dev = diag.shape[1]
    row_blocks = rows_dev // BLOCK
    rows_here = kids.shape[2]
    vmem, smem = pl.BlockSpec(memory_space=pltpu.VMEM), pl.BlockSpec(memory_space=pltpu.SMEM)
    anywhere = pl.BlockSpec(memory_space=pl.ANY)

    def along(x, by):
        return lax.ppermute(x, "row", [(i, (i + 2 * by) % n_row) for i in range(n_row)])

    def partner(x):
        return lax.ppermute(x, "row", [(i, i ^ 1) for i in range(n_row)])

    def parent(x, by):
        pairs = []
        for f in range(fronts):
            for i in range(n_row):
                pairs.append((f * n_row + i, (f - 1) % fronts * n_row + (i + 2 * by) % n_row))
        return lax.ppermute(x, ("front", "row"), pairs)

    def neighbour(x):
        return lax.ppermute(x, "col", [(i, i ^ 1) for i in range(n_col)])

    lines = 3 * BLOCK + 16
    maps = jnp.swapaxes(maps, 2, 3)
    mask = jnp.swapaxes(mask, 1, 2)
    side = lines + 2 * rows_here
    shapes = [side, rows_here, lines, side, 2 * rows_here, rows_here]
    shapes = [jax.ShapeDtypeStruct((size, BLOCK), BF16) for size in shapes]
    shapes = [jax.ShapeDtypeStruct((2, maps.shape[3]), jnp.int32)] + shapes
    tables, own_side, own_rest, far_window, far_side, far_pair, far_column = pl.pallas_call(
        select_kernel,
        out_shape=shapes,
        in_specs=[vmem, vmem, pl.BlockSpec(memory_space=pltpu.HBM)],
        out_specs=[vmem] * len(shapes),
        scratch_shapes=[pltpu.SemaphoreType.DMA((22,))],
        compiler_params=params(55),
        cost_estimate=cost(2),
        name="select",
    )(maps, diag, kids)

    def both(x):
        return x, partner(x)

    far_windows = [parent(far_window, s) for s in range(1, chips)]
    own_sides = [along(own_side, s) for s in range(1, chips)]
    far_near = parent(far_side, 0)
    far_windows, own_sides, far_near, own_side = lax.optimization_barrier(
        (far_windows, own_sides, far_near, own_side)
    )
    far_windows = [both(x) for x in far_windows]
    own_sides = [both(own_side)] + [both(x) for x in own_sides]
    far_near = both(far_near)
    far_pairs = [parent(far_pair, s) for s in range(1, chips)]
    far_columns = [parent(far_column, s) for s in range(1, chips)]
    middle = slice(lines, lines + rows_here)
    own_others = [neighbour(x[middle]) for x, _ in own_sides[1:]]
    far_other = neighbour(far_near[0][middle])
    own_parts = [x for pair in own_sides for x in pair]
    far_parts = list(far_near) + [x for pair in far_windows for x in pair]
    far_table = far_near[0][3 * BLOCK, : tables.shape[1]].astype(jnp.int32)
    inverse = pl.pallas_call(
        functools.partial(factor_kernel, len(own_parts)),
        out_shape=jax.ShapeDtypeStruct((NPANEL * PW, NPANEL * PW), F32),
        compiler_params=params(),
        cost_estimate=cost(0),
        name="factor",
    )(*own_parts, *far_parts)

    remote = (own_rest, own_others, far_other, far_pairs, far_columns)
    remote, inverse = lax.optimization_barrier((remote, inverse))
    own_rest, own_others, far_other, far_pairs, far_columns = remote

    def owner(side, s):
        def position(me):
            core = me + 1 - 2 * (me % 2) if side else me
            return (core + n_row - 2 * s) % n_row

        return position

    pairs, columns, arrays, column_arrays = [], [], [], []

    def add(child, s, first, second, column, at):
        for core in range(2):
            pairs.append((child, owner(core, s), second is None))
            arrays.extend([first[core]] if second is None else [first[core], second[core]])
            columns.append((child, owner(core, s), at))
            column_arrays.append(column[core])

    at = lines + rows_here
    add(0, 0, own_sides[0], both(own_rest), own_sides[0], at)
    add(1, 0, far_near, both(far_other), far_near, at)
    for s in range(1, chips):
        add(0, s, own_sides[s], both(own_others[s - 1]), own_sides[s], at)
        add(1, s, both(far_pairs[s - 1]), None, both(far_columns[s - 1]), 0)

    tables = jnp.stack([tables[0], far_table])
    height = n_row * rows_here + BLOCK
    weight, product = pl.pallas_call(
        functools.partial(product_kernel, pairs, n_row, lines),
        out_shape=[
            jax.ShapeDtypeStruct((NPANEL * PW, PW), F32),
            jax.ShapeDtypeStruct((2, height, PW), F32),
        ],
        in_specs=[smem] + [vmem] * (1 + len(arrays)),
        out_specs=[vmem, vmem],
        compiler_params=params(),
        cost_estimate=cost(3),
        name="product",
    )(tables, inverse, *arrays)

    return pl.pallas_call(
        functools.partial(front_kernel, columns, n_row, row_blocks),
        out_shape=jax.ShapeDtypeStruct((1, rows_dev, PW), F32),
        in_specs=[smem, smem] + [vmem] * (3 + len(column_arrays)),
        out_specs=vmem,
        scratch_shapes=[pltpu.VMEM((2, height, PW), BF16)],
        compiler_params=params(),
        cost_estimate=cost(2),
        name="front",
    )(tables, mask, diag, weight, product, *column_arrays)


def solution(mesh):
    in_specs = (
        P("front", None, "row", None),
        P("front", None, None, None),
        P("front", None, None),
        P("front", "row"),
    )
    out_specs = P("front", "row", "col")
    return jax.shard_map(body, mesh=mesh, in_specs=in_specs, out_specs=out_specs, check_vma=False)
```

```python
import functools

import jax
import jax.numpy as jnp
from jax import lax
from jax.experimental import pallas as pl
from jax.experimental.pallas import tpu as pltpu
from jax.sharding import PartitionSpec as P

BLOCK = 128
PW = 128
NPANEL = 2
F32 = jnp.float32
BF16 = jnp.bfloat16
HIGHEST = lax.Precision.HIGHEST
MIB = 1024 * 1024


def params(mib=40):
    return pltpu.CompilerParams(vmem_limit_bytes=mib * MIB)


def copy_columns(kids, sems, copies, found, child, p, start, size, target, here=None):
    none = kids.shape[3] // BLOCK
    col = found[child][p]
    here = (col < none) if here is None else here & (col < none)
    start = pl.multiple_of(jnp.where(here, start, 0), 16)
    col = pl.multiple_of(jnp.where(here, col, 0) * BLOCK, BLOCK)
    source = kids.at[0, child, pl.ds(start, size), pl.ds(col, BLOCK)]
    copy = pltpu.make_async_copy(source, target, sems.at[len(copies)])
    copies.append((here, copy))

    @pl.when(here)
    def _():
        copy.start()

    @pl.when(jnp.logical_not(here))
    def _():
        target[...] = jnp.zeros_like(target)


def finish(copies):
    for here, copy in copies:

        @pl.when(here)
        def _():
            copy.wait()


def select_kernel(maps_hbm, diag_hbm, kids, tables, own_side, far_window, far_side, maps, diag, sems):
    first = pltpu.make_async_copy(maps_hbm, maps, sems.at[sems.shape[0] - 2])
    second = pltpu.make_async_copy(diag_hbm, diag, sems.at[sems.shape[0] - 1])
    first.start()
    second.start()
    me, col_index = lax.axis_index("row"), lax.axis_index("col")
    rows = kids.shape[2]
    local = rows // BLOCK
    none = kids.shape[3] // BLOCK
    lines = far_window.shape[0]
    places = maps.shape[3]
    child_id = lax.broadcasted_iota(jnp.int32, (none, places), 0)
    place_id = lax.broadcasted_iota(jnp.int32, (1, places), 1)
    found = []
    first.wait()
    for child in range(2):
        ones = maps[0, child].astype(F32)
        line = jnp.sum(ones * (child_id - none).astype(F32), axis=0, keepdims=True) + none
        tables[child : child + 1, :] = line.astype(jnp.int32)
        found.append(
            [
                jnp.sum(jnp.where(place_id == w, line, 0.0)).astype(jnp.int32)
                for w in (0, 1, col_index)
            ]
        )
        if child == 1:
            line = jnp.broadcast_to(line, (16, places)).astype(BF16)
            far_side[3 * BLOCK : lines, 0:places] = line
            far_window[3 * BLOCK :, 0:places] = line
    copies = []
    for child, out in ((1, far_window), (0, own_side), (1, far_side)):
        for at, (w, p) in enumerate(((0, 0), (1, 0), (1, 1))):
            row = found[child][w]
            offset = row - me * local
            here = (row < none) & (offset >= 0) & (offset < local)
            target = out.at[pl.ds(at * BLOCK, BLOCK)]
            copy_columns(kids, sems, copies, found, child, p, offset * BLOCK, BLOCK, target, here)
    half = rows // 2
    for child, out in ((0, own_side), (1, far_side)):
        for p in range(NPANEL):
            target = out.at[pl.ds(lines + p * half, half)]
            copy_columns(kids, sems, copies, found, child, p, col_index % 2 * half, half, target)
        target = out.at[pl.ds(lines + rows, rows)]
        copy_columns(kids, sems, copies, found, child, NPANEL, 0, rows, target)

    second.wait()
    line = lax.broadcasted_iota(jnp.int32, (16, BLOCK), 0)
    pieces = jnp.zeros((16, BLOCK), F32)
    for p in range(NPANEL):
        rest = jnp.broadcast_to(diag[0:1, p * PW : (p + 1) * PW], (16, BLOCK))
        for at in range(3):
            part = rest.astype(BF16).astype(F32)
            pieces = jnp.where(line == 3 * p + at, part, pieces)
            rest = rest - part
    own_side[3 * BLOCK : lines, :] = jnp.where(me == 0, pieces, 0.0).astype(BF16)
    finish(copies)


def remain_kernel(tables, kids, far_all, own_rest, sems):
    col_index = lax.axis_index("col")
    rows = kids.shape[2]
    half = rows // 2
    here, other = col_index % 2 * half, (1 - col_index % 2) * half
    found = [[tables[child, w] for w in (0, 1, col_index)] for child in range(2)]
    copies = []
    for child, out, parts in (
        (
            1,
            far_all,
            [(0, here, half), (1, here, half), (0, other, half), (1, other, half), (2, 0, rows)],
        ),
        (0, own_rest, [(0, other, half), (1, other, half)]),
    ):
        at = 0
        for p, start, size in parts:
            target = out.at[pl.ds(at, size)]
            copy_columns(kids, sems, copies, found, child, p, start, size, target)
            at += size
    finish(copies)


def cost(microseconds):
    return pl.CostEstimate(flops=microseconds * 10**9, bytes_accessed=0, transcendentals=0)


def inverse_factor(tiles):
    tiles = list(tiles)
    count = len(tiles)
    lane = lax.broadcasted_iota(jnp.int32, (8, BLOCK), 1)
    line = lax.broadcasted_iota(jnp.int32, (8, BLOCK), 0)
    wide = lambda x: jnp.broadcast_to(x, (8, BLOCK))
    result = []
    for b in range(count):
        low = 8 * b
        tile = tiles[b]
        columns = [wide(tile[:, low + j : low + j + 1]) for j in range(8)]
        d = [[wide(columns[j][i : i + 1, :]) if i >= j else None for j in range(8)] for i in range(8)]
        inside = (lane >= low) & (lane < low + 8)
        rows = [
            jnp.where(inside, (lane == low + i).astype(F32), wide(tile[i : i + 1, :]))
            for i in range(8)
        ]
        scale = []
        for j in range(8):
            scale.append(lax.rsqrt(d[j][j]))
            for i in range(j + 1, 8):
                d[i][j] = d[i][j] * scale[j]
            for k in range(j + 1, 8):
                for i in range(k, 8):
                    d[i][k] = d[i][k] - d[i][j] * d[k][j]
            rows[j] = rows[j] * scale[j]
            for i in range(j + 1, 8):
                rows[i] = rows[i] - d[i][j] * rows[j]
        merged = rows[0]
        for j in range(1, 8):
            merged = jnp.where(line == j, rows[j], merged)
        result.append(jnp.where(lane < low + 8, merged, 0.0))
        for t in range(b + 1, count):
            tile = tiles[t]
            columns = [wide(tile[:, low + j : low + j + 1]) for j in range(8)]
            tile = jnp.where(inside, 0.0, tile)
            for j in range(8):
                for m in range(j):
                    columns[j] = columns[j] - columns[m] * d[j][m]
                columns[j] = columns[j] * scale[j]
                tile = tile - columns[j] * rows[j]
            tiles[t] = tile
    return result


def dot(a, b, lhs=1, rhs=0):
    return lax.dot_general(
        a, b, (((lhs,), (rhs,)), ((), ())), precision=HIGHEST, preferred_element_type=F32
    )


def invert(block):
    tiles = [block[8 * t : 8 * t + 8, :] for t in range(BLOCK // 8)]
    return jnp.concatenate(inverse_factor(tiles), axis=0)


def first_kernel(n_own, *refs):
    own, far = refs[:n_own], refs[n_own:-3]
    inverse, below, rest = refs[-3:]

    def total(at):
        value = None
        for ref in own + far:
            block = ref[at * BLOCK : (at + 1) * BLOCK, :].astype(F32)
            value = block if value is None else value + block
        return value

    pieces = None
    for ref in own:
        part = ref[3 * BLOCK : 3 * BLOCK + 16, :].astype(F32)
        pieces = part if pieces is None else pieces + part
    eye = lax.broadcasted_iota(jnp.int32, (BLOCK, BLOCK), 0) == lax.broadcasted_iota(
        jnp.int32, (BLOCK, BLOCK), 1
    )

    def diagonal(p):
        line = pieces[3 * p : 3 * p + 1] + pieces[3 * p + 1 : 3 * p + 2]
        line = line + pieces[3 * p + 2 : 3 * p + 3]
        return jnp.where(eye, jnp.broadcast_to(line, (BLOCK, BLOCK)), 0.0)

    inverse[...] = invert(total(0) + diagonal(0))
    below[...] = dot(total(1), inverse[...], 1, 1)
    rest[...] = total(2) + diagonal(1) - dot(below[...], below[...], 1, 1)


def second_kernel(first, below, rest, out):
    inverse = invert(rest[...])
    out[0:BLOCK, 0:BLOCK] = first[...]
    out[0:BLOCK, BLOCK:] = jnp.zeros((BLOCK, BLOCK), F32)
    out[BLOCK:, 0:BLOCK] = -dot(inverse, dot(below[...], first[...]))
    out[BLOCK:, BLOCK:] = inverse


def front_kernel(layout, n_row, row_blocks, tables, mask, diag, inverse, *refs):
    out, weight, product, buffer = refs[-4:]
    me, col_index = lax.axis_index("row"), lax.axis_index("col")
    is_panel = col_index < NPANEL
    rows = (product.shape[1] - BLOCK) // n_row
    half = rows // 2
    wide = NPANEL * PW
    parts = []
    for child, owner, (first, start), (second, at), column in layout:
        parts.append((child, owner(me), refs[first], start, col_index % 2))
        parts.append((child, owner(me), refs[second], at, 1 - col_index % 2))
        start = pl.multiple_of(owner(me) * rows, rows)
        buffer[child, pl.ds(start, rows), :] = refs[first][column : column + rows, :]

    mirrored = jnp.zeros((BLOCK, wide), F32)
    for child, owner, ref, at, side in parts:
        index = tables[child, col_index] * BLOCK
        for step in range(0, BLOCK, BLOCK // 2):
            place = index + step - owner * rows - side * half
            inside = (place >= 0) & (place < half)
            place = pl.multiple_of(jnp.where(inside, place, 0), BLOCK // 2)
            lines = [ref[pl.ds(at + p * half + place, BLOCK // 2), :] for p in range(NPANEL)]
            lines = jnp.where(inside, jnp.concatenate(lines, axis=1).astype(F32), 0.0)
            empty = jnp.zeros_like(lines)
            lines = [lines, empty] if step == 0 else [empty, lines]
            mirrored = mirrored + jnp.concatenate(lines, axis=0)

    lower = inverse[...]
    row_id = lax.broadcasted_iota(jnp.int32, (wide, PW), 0)
    col_id = lax.broadcasted_iota(jnp.int32, (wide, PW), 1)
    picked = -(row_id == col_id + col_index * PW).astype(F32)
    solved = jnp.where(is_panel, picked, dot(lower, mirrored, 1, 1))
    weight[...] = dot(lower, solved, 0, 0)
    high = weight[...].astype(BF16)
    low = (weight[...] - high.astype(F32)).astype(BF16)
    both = jnp.concatenate([high, low], axis=1)
    for child, owner, ref, at, side in parts:
        left = jnp.concatenate(
            [ref[at + p * half : at + (p + 1) * half, :] for p in range(NPANEL)], axis=1
        )
        value = jnp.dot(left, both, preferred_element_type=F32)
        start = pl.multiple_of(owner * rows + side * half, half)
        product[child, pl.ds(start, half), :] = value[:, :PW] + value[:, PW:]
    for child in range(2):
        product[child, n_row * rows :, :] = jnp.zeros((BLOCK, PW), F32)
        buffer[child, n_row * rows :, :] = jnp.zeros((BLOCK, PW), BF16)

    for p in range(row_blocks):
        at = me * row_blocks + p
        first, second = (
            pl.ds(pl.multiple_of(tables[child, at] * BLOCK, BLOCK), BLOCK) for child in range(2)
        )
        base = buffer[0, first, :].astype(F32) + buffer[1, second, :].astype(F32)
        keep = jnp.where(is_panel | (mask[0, col_index, at] > 0), 1.0, 0.0)
        value = jnp.where(is_panel, 0.0, base) - keep * (product[0, first, :] + product[1, second, :])
        out[0, p * BLOCK : (p + 1) * BLOCK, :] = value

    row_id = lax.broadcasted_iota(jnp.int32, (BLOCK, BLOCK), 0)
    col_id = lax.broadcasted_iota(jnp.int32, (BLOCK, BLOCK), 1)

    def diagonal(p):
        line = jnp.broadcast_to(diag[0:1, p * BLOCK : (p + 1) * BLOCK], (BLOCK, BLOCK))
        return jnp.where(row_id == col_id, line, 0.0)

    for p in range(NPANEL):

        @pl.when(me == 0)
        def _():
            keep = jnp.where(is_panel | (mask[0, col_index, p] > 0), 1.0, 0.0)
            column = jnp.sum(diagonal(p), axis=1, keepdims=True)
            value = out[0, p * BLOCK : (p + 1) * BLOCK, :]
            value = value - keep * column * weight[p * BLOCK : (p + 1) * BLOCK, :]
            above = row_id + p * BLOCK < col_id + col_index * PW
            out[0, p * BLOCK : (p + 1) * BLOCK, :] = jnp.where(is_panel & above, 0.0, value)

    for p in range(row_blocks):

        @pl.when(jnp.logical_not(is_panel) & (me * row_blocks + p == col_index))
        def _():
            out[0, p * BLOCK : (p + 1) * BLOCK, :] += diagonal(p)


def body(kids, maps, mask, diag):
    fronts, n_row, n_col = (lax.axis_size(name) for name in ("front", "row", "col"))
    chips = n_row // 2
    rows_dev = diag.shape[1]
    row_blocks = rows_dev // BLOCK
    rows_here = kids.shape[2]
    vmem, smem = pl.BlockSpec(memory_space=pltpu.VMEM), pl.BlockSpec(memory_space=pltpu.SMEM)
    anywhere = pl.BlockSpec(memory_space=pl.ANY)

    def along(x, by):
        return lax.ppermute(x, "row", [(i, (i + 2 * by) % n_row) for i in range(n_row)])

    def partner(x):
        return lax.ppermute(x, "row", [(i, i ^ 1) for i in range(n_row)])

    def parent(x, by):
        pairs = []
        for f in range(fronts):
            for i in range(n_row):
                pairs.append((f * n_row + i, (f - 1) % fronts * n_row + (i + 2 * by) % n_row))
        return lax.ppermute(x, ("front", "row"), pairs)

    def neighbour(x):
        return lax.ppermute(x, "col", [(i, i ^ 1) for i in range(n_col)])

    lines = 3 * BLOCK + 16
    maps = jnp.swapaxes(maps, 2, 3)
    mask = jnp.swapaxes(mask, 1, 2)
    def shapes(*sizes):
        return [jax.ShapeDtypeStruct((size, BLOCK), BF16) for size in sizes]

    def both(x):
        return x, partner(x)

    hbm = pl.BlockSpec(memory_space=pltpu.HBM)
    kids = pltpu.with_memory_space_constraint(kids, pltpu.HBM)
    diag_hbm = pltpu.with_memory_space_constraint(diag, pltpu.HBM)
    tables, own_side, far_window, far_side = pl.pallas_call(
        select_kernel,
        out_shape=[jax.ShapeDtypeStruct((2, maps.shape[3]), jnp.int32)]
        + shapes(lines + 2 * rows_here, lines, lines + 2 * rows_here),
        in_specs=[hbm] * 3,
        out_specs=[vmem] * 4,
        scratch_shapes=[
            pltpu.VMEM(maps.shape, jnp.int32),
            pltpu.VMEM(diag.shape, F32),
            pltpu.SemaphoreType.DMA((17,)),
        ],
        compiler_params=params(),
        cost_estimate=cost(0),
        name="select",
    )(pltpu.with_memory_space_constraint(maps, pltpu.HBM), diag_hbm, kids)
    far_all, own_rest = pl.pallas_call(
        remain_kernel,
        out_shape=shapes(3 * rows_here, rows_here),
        in_specs=[smem, hbm],
        out_specs=[vmem] * 2,
        scratch_shapes=[pltpu.SemaphoreType.DMA((7,))],
        compiler_params=params(),
        cost_estimate=cost(0),
        name="remain",
    )(tables, kids)

    far_windows = [parent(far_window, s) for s in range(1, chips)]
    own_sides = [along(own_side, s) for s in range(1, chips)]
    far_near = parent(far_side, 0)
    arrived = (far_windows, own_sides, far_near, own_side, far_all)
    arrived = lax.optimization_barrier(arrived)
    far_windows, own_sides, far_near, own_side, far_all = arrived
    far_windows = [both(x) for x in far_windows]
    own_sides = [both(own_side)] + [both(x) for x in own_sides]
    far_near = both(far_near)
    far_alls = [parent(far_all, s) for s in range(1, chips)]
    own_parts = [x for pair in own_sides for x in pair]
    far_parts = list(far_near) + [x for pair in far_windows for x in pair]
    middle = slice(lines, lines + rows_here)
    halves = [x[middle] for x, _ in own_sides[1:]] + [far_near[0][middle]]
    others = neighbour(jnp.concatenate(halves, axis=0))
    far_table = far_near[0][3 * BLOCK, : tables.shape[1]].astype(jnp.int32)
    square = jax.ShapeDtypeStruct((BLOCK, BLOCK), F32)
    first = pl.pallas_call(
        functools.partial(first_kernel, len(own_parts)),
        out_shape=[square] * 3,
        compiler_params=params(),
        cost_estimate=cost(0),
        name="first_factor",
    )(*own_parts, *far_parts)
    inverse = pl.pallas_call(
        second_kernel,
        out_shape=jax.ShapeDtypeStruct((NPANEL * PW, NPANEL * PW), F32),
        compiler_params=params(),
        cost_estimate=cost(0),
        name="second_factor",
    )(*first)

    remote = (own_rest, others, far_alls)
    remote, inverse = lax.optimization_barrier((remote, inverse))
    own_rest, others, far_alls = remote
    own_rest, others = both(own_rest), both(others)

    def owner(side, s):
        def position(me):
            core = me + 1 - 2 * (me % 2) if side else me
            return (core + n_row - 2 * s) % n_row

        return position

    layout, arrays = [], list(others)

    def add(child, s, first, second):
        for core in range(2):
            if isinstance(second, int):
                rest = (core, second * rows_here)
            else:
                rest = (len(arrays) + 1, 0) if second else (len(arrays), rows_here)
            start = lines if second is not None else 0
            column = start + rows_here if second is not None else 2 * rows_here
            layout.append((child, owner(core, s), (len(arrays), start), rest, column))
            arrays.append(first[core])
            if isinstance(second, tuple):
                arrays.append(second[core])

    far_alls = [both(x) for x in far_alls]
    add(0, 0, own_sides[0], own_rest)
    add(1, 0, far_near, chips - 1)
    for s in range(1, chips):
        add(0, s, own_sides[s], s - 1)
        add(1, s, far_alls[s - 1], None)

    tables = jnp.stack([tables[0], far_table])
    height = n_row * rows_here + BLOCK
    return pl.pallas_call(
        functools.partial(front_kernel, layout, n_row, row_blocks),
        out_shape=jax.ShapeDtypeStruct((1, rows_dev, PW), F32),
        in_specs=[smem, smem] + [vmem] * (2 + len(arrays)),
        out_specs=vmem,
        scratch_shapes=[
            pltpu.VMEM((NPANEL * PW, PW), F32),
            pltpu.VMEM((2, height, PW), F32),
            pltpu.VMEM((2, height, PW), BF16),
        ],
        compiler_params=params(),
        cost_estimate=cost(0),
        name="front",
    )(tables, mask, diag, inverse, *arrays)


def solution(mesh):
    in_specs = (
        P("front", None, "row", None),
        P("front", None, None, None),
        P("front", None, None),
        P("front", "row"),
    )
    out_specs = P("front", "row", "col")
    return jax.shard_map(body, mesh=mesh, in_specs=in_specs, out_specs=out_specs, check_vma=False)
```

```python
import functools

import jax
import jax.numpy as jnp
from jax import lax
from jax.experimental import pallas as pl
from jax.experimental.pallas import tpu as pltpu
from jax.sharding import PartitionSpec as P

BLOCK = 128
PW = 128
NPANEL = 2
F32 = jnp.float32
BF16 = jnp.bfloat16
HIGHEST = lax.Precision.HIGHEST
NOTES = 2 * BLOCK
WINDOW = NOTES + 16
MIB = 1024 * 1024


def params(mib=40):
    return pltpu.CompilerParams(vmem_limit_bytes=mib * MIB)


def copy_columns(kids, sems, copies, found, child, p, start, size, target, here=None):
    none = kids.shape[3] // BLOCK
    col = found[child][p]
    here = (col < none) if here is None else here & (col < none)
    start = pl.multiple_of(jnp.where(here, start, 0), 16)
    col = pl.multiple_of(jnp.where(here, col, 0) * BLOCK, BLOCK)
    source = kids.at[0, child, pl.ds(start, size), pl.ds(col, BLOCK)]
    copy = pltpu.make_async_copy(source, target, sems.at[len(copies)])
    copies.append((here, copy))

    @pl.when(here)
    def _():
        copy.start()

    @pl.when(jnp.logical_not(here))
    def _():
        target[...] = jnp.zeros_like(target)


def finish(copies):
    for here, copy in copies:

        @pl.when(here)
        def _():
            copy.wait()


def select_kernel(maps_hbm, diag_hbm, kids, tables, own_side, far_window, far_side, maps, diag, corner, sems):
    first = pltpu.make_async_copy(maps_hbm, maps, sems.at[sems.shape[0] - 2])
    second = pltpu.make_async_copy(diag_hbm, diag, sems.at[sems.shape[0] - 1])
    first.start()
    second.start()
    me, col_index = lax.axis_index("row"), lax.axis_index("col")
    rows = kids.shape[2]
    local = rows // BLOCK
    none = kids.shape[3] // BLOCK
    lines = far_window.shape[0]
    places = maps.shape[3]
    child_id = lax.broadcasted_iota(jnp.int32, (none, places), 0)
    place_id = lax.broadcasted_iota(jnp.int32, (1, places), 1)
    found = []
    first.wait()
    for child in range(2):
        ones = maps[0, child].astype(F32)
        line = jnp.sum(ones * (child_id - none).astype(F32), axis=0, keepdims=True) + none
        tables[child : child + 1, :] = line.astype(jnp.int32)
        found.append(
            [
                jnp.sum(jnp.where(place_id == w, line, 0.0)).astype(jnp.int32)
                for w in (0, 1, col_index)
            ]
        )
        if child == 1:
            line = jnp.broadcast_to(line, (16, places)).astype(BF16)
            table = jnp.concatenate([line, jnp.zeros((16, BLOCK - places), BF16)], axis=1)
    copies = []
    for child, out in ((0, own_side), (1, far_side)):
        targets = (out.at[pl.ds(0, BLOCK)], out.at[pl.ds(BLOCK, BLOCK)], corner.at[child])
        for (w, p), target in zip(((0, 0), (1, 0), (1, 1)), targets):
            row = found[child][w]
            offset = row - me * local
            here = (row < none) & (offset >= 0) & (offset < local)
            copy_columns(kids, sems, copies, found, child, p, offset * BLOCK, BLOCK, target, here)
    corners = list(copies)
    half = rows // 2
    for child, out in ((0, own_side), (1, far_side)):
        for p in range(NPANEL):
            target = out.at[pl.ds(lines + p * half, half)]
            copy_columns(kids, sems, copies, found, child, p, col_index % 2 * half, half, target)
        target = out.at[pl.ds(lines + rows, rows)]
        copy_columns(kids, sems, copies, found, child, NPANEL, 0, rows, target)

    second.wait()
    line = lax.broadcasted_iota(jnp.int32, (16, BLOCK), 0)
    pieces = jnp.zeros((16, BLOCK), F32)
    for p in range(NPANEL):
        rest = jnp.broadcast_to(diag[0:1, p * PW : (p + 1) * PW], (16, BLOCK))
        for at in range(3):
            part = rest.astype(BF16).astype(F32)
            pieces = jnp.where(line == 3 * p + at, part, pieces)
            rest = rest - part
    pieces = jnp.where(me == 0, pieces, 0.0)
    finish(corners)
    row_id = lax.broadcasted_iota(jnp.int32, (BLOCK, BLOCK), 0)
    col_id = lax.broadcasted_iota(jnp.int32, (BLOCK, BLOCK), 1)
    for child, out in ((0, own_side), (1, far_side)):
        upper = corner[child].astype(F32)
        lower = out[0:BLOCK, :].astype(F32)
        out[0:BLOCK, :] = jnp.where(row_id >= col_id, lower, upper).astype(BF16)
        middle = jnp.sum(jnp.where(row_id == col_id, upper, 0.0), axis=0, keepdims=True)
        notes = jnp.where(line == 6, jnp.broadcast_to(middle, (16, BLOCK)), 0.0)
        notes = notes + pieces if child == 0 else jnp.where(line == 7, table.astype(F32), notes)
        out[NOTES:lines, :] = notes.astype(BF16)
    far_window[...] = far_side[0:lines, :]
    finish(copies[len(corners) :])


def remain_kernel(tables, kids, far_all, own_rest, sems):
    col_index = lax.axis_index("col")
    rows = kids.shape[2]
    half = rows // 2
    here, other = col_index % 2 * half, (1 - col_index % 2) * half
    found = [[tables[child, w] for w in (0, 1, col_index)] for child in range(2)]
    copies = []
    for child, out, parts in (
        (
            1,
            far_all,
            [(0, here, half), (1, here, half), (0, other, half), (1, other, half), (2, 0, rows)],
        ),
        (0, own_rest, [(0, other, half), (1, other, half)]),
    ):
        at = 0
        for p, start, size in parts:
            target = out.at[pl.ds(at, size)]
            copy_columns(kids, sems, copies, found, child, p, start, size, target)
            at += size
    finish(copies)


def cost(microseconds):
    return pl.CostEstimate(flops=microseconds * 10**9, bytes_accessed=0, transcendentals=0)


def inverse_factor(tiles):
    tiles = list(tiles)
    count = len(tiles)
    lane = lax.broadcasted_iota(jnp.int32, (8, BLOCK), 1)
    line = lax.broadcasted_iota(jnp.int32, (8, BLOCK), 0)
    wide = lambda x: jnp.broadcast_to(x, (8, BLOCK))
    result = []
    for b in range(count):
        low = 8 * b
        tile = tiles[b]
        columns = [wide(tile[:, low + j : low + j + 1]) for j in range(8)]
        d = [[wide(columns[j][i : i + 1, :]) if i >= j else None for j in range(8)] for i in range(8)]
        inside = (lane >= low) & (lane < low + 8)
        rows = [
            jnp.where(inside, (lane == low + i).astype(F32), wide(tile[i : i + 1, :]))
            for i in range(8)
        ]
        scale = []
        for j in range(8):
            scale.append(lax.rsqrt(d[j][j]))
            for i in range(j + 1, 8):
                d[i][j] = d[i][j] * scale[j]
            for k in range(j + 1, 8):
                for i in range(k, 8):
                    d[i][k] = d[i][k] - d[i][j] * d[k][j]
            rows[j] = rows[j] * scale[j]
            for i in range(j + 1, 8):
                rows[i] = rows[i] - d[i][j] * rows[j]
        merged = rows[0]
        for j in range(1, 8):
            merged = jnp.where(line == j, rows[j], merged)
        result.append(jnp.where(lane < low + 8, merged, 0.0))
        for t in range(b + 1, count):
            tile = tiles[t]
            columns = [wide(tile[:, low + j : low + j + 1]) for j in range(8)]
            tile = jnp.where(inside, 0.0, tile)
            for j in range(8):
                for m in range(j):
                    columns[j] = columns[j] - columns[m] * d[j][m]
                columns[j] = columns[j] * scale[j]
                tile = tile - columns[j] * rows[j]
            tiles[t] = tile
    return result


def dot(a, b, lhs=1, rhs=0):
    return lax.dot_general(
        a, b, (((lhs,), (rhs,)), ((), ())), precision=HIGHEST, preferred_element_type=F32
    )


def invert(block):
    tiles = [block[8 * t : 8 * t + 8, :] for t in range(BLOCK // 8)]
    return jnp.concatenate(inverse_factor(tiles), axis=0)


def first_kernel(n_own, *refs):
    own, far = refs[:n_own], refs[n_own:-3]
    inverse, below, rest = refs[-3:]

    def total(group, start, size):
        value = None
        for ref in group:
            part = ref[start : start + size, :].astype(F32)
            value = part if value is None else value + part
        return value

    row_id = lax.broadcasted_iota(jnp.int32, (BLOCK, BLOCK), 0)
    col_id = lax.broadcasted_iota(jnp.int32, (BLOCK, BLOCK), 1)
    own_notes, far_notes = total(own, NOTES, 16), total(far, NOTES, 16)

    def diagonal(line):
        return jnp.where(row_id == col_id, jnp.broadcast_to(line, (BLOCK, BLOCK)), 0.0)

    def initial(p):
        line = own_notes[3 * p : 3 * p + 1] + own_notes[3 * p + 1 : 3 * p + 2]
        return line + own_notes[3 * p + 2 : 3 * p + 3]

    corners = total(own + far, 0, BLOCK)
    lower = jnp.where(row_id > col_id, corners, 0.0)
    middle = jnp.where(row_id == col_id, corners, 0.0)
    upper = jnp.where(row_id < col_id, corners, 0.0)
    inverse[...] = invert(lower + lower.T + middle + diagonal(initial(0)))
    below[...] = dot(total(own + far, BLOCK, BLOCK), inverse[...], 1, 1)
    line = own_notes[6:7] + far_notes[6:7] + initial(1)
    rest[...] = upper + upper.T + diagonal(line) - dot(below[...], below[...], 1, 1)


def second_kernel(first, below, rest, out):
    inverse = invert(rest[...])
    out[0:BLOCK, 0:BLOCK] = first[...]
    out[0:BLOCK, BLOCK:] = jnp.zeros((BLOCK, BLOCK), F32)
    out[BLOCK:, 0:BLOCK] = -dot(inverse, dot(below[...], first[...]))
    out[BLOCK:, BLOCK:] = inverse


def front_kernel(layout, n_row, row_blocks, tables, mask, diag, inverse, *refs):
    out, weight, product, buffer = refs[-4:]
    me, col_index = lax.axis_index("row"), lax.axis_index("col")
    is_panel = col_index < NPANEL
    rows = (product.shape[1] - BLOCK) // n_row
    half = rows // 2
    wide = NPANEL * PW
    parts = []
    for child, owner, (first, start), (second, at), column in layout:
        parts.append((child, owner(me), refs[first], start, col_index % 2))
        parts.append((child, owner(me), refs[second], at, 1 - col_index % 2))
        start = pl.multiple_of(owner(me) * rows, rows)
        buffer[child, pl.ds(start, rows), :] = refs[first][column : column + rows, :]

    mirrored = jnp.zeros((BLOCK, wide), F32)
    for child, owner, ref, at, side in parts:
        index = tables[child, col_index] * BLOCK
        for step in range(0, BLOCK, BLOCK // 2):
            place = index + step - owner * rows - side * half
            inside = (place >= 0) & (place < half)
            place = pl.multiple_of(jnp.where(inside, place, 0), BLOCK // 2)
            lines = [ref[pl.ds(at + p * half + place, BLOCK // 2), :] for p in range(NPANEL)]
            lines = jnp.where(inside, jnp.concatenate(lines, axis=1).astype(F32), 0.0)
            empty = jnp.zeros_like(lines)
            lines = [lines, empty] if step == 0 else [empty, lines]
            mirrored = mirrored + jnp.concatenate(lines, axis=0)

    lower = inverse[...]
    row_id = lax.broadcasted_iota(jnp.int32, (wide, PW), 0)
    col_id = lax.broadcasted_iota(jnp.int32, (wide, PW), 1)
    picked = -(row_id == col_id + col_index * PW).astype(F32)
    solved = jnp.where(is_panel, picked, dot(lower, mirrored, 1, 1))
    weight[...] = dot(lower, solved, 0, 0)
    high = weight[...].astype(BF16)
    low = (weight[...] - high.astype(F32)).astype(BF16)
    both = jnp.concatenate([high, low], axis=1)
    for child, owner, ref, at, side in parts:
        left = jnp.concatenate(
            [ref[at + p * half : at + (p + 1) * half, :] for p in range(NPANEL)], axis=1
        )
        value = jnp.dot(left, both, preferred_element_type=F32)
        start = pl.multiple_of(owner * rows + side * half, half)
        product[child, pl.ds(start, half), :] = value[:, :PW] + value[:, PW:]
    for child in range(2):
        product[child, n_row * rows :, :] = jnp.zeros((BLOCK, PW), F32)
        buffer[child, n_row * rows :, :] = jnp.zeros((BLOCK, PW), BF16)

    for p in range(row_blocks):
        at = me * row_blocks + p
        first, second = (
            pl.ds(pl.multiple_of(tables[child, at] * BLOCK, BLOCK), BLOCK) for child in range(2)
        )
        base = buffer[0, first, :].astype(F32) + buffer[1, second, :].astype(F32)
        keep = jnp.where(is_panel | (mask[0, col_index, at] > 0), 1.0, 0.0)
        value = jnp.where(is_panel, 0.0, base) - keep * (product[0, first, :] + product[1, second, :])
        out[0, p * BLOCK : (p + 1) * BLOCK, :] = value

    row_id = lax.broadcasted_iota(jnp.int32, (BLOCK, BLOCK), 0)
    col_id = lax.broadcasted_iota(jnp.int32, (BLOCK, BLOCK), 1)

    def diagonal(p):
        line = jnp.broadcast_to(diag[0:1, p * BLOCK : (p + 1) * BLOCK], (BLOCK, BLOCK))
        return jnp.where(row_id == col_id, line, 0.0)

    for p in range(NPANEL):

        @pl.when(me == 0)
        def _():
            keep = jnp.where(is_panel | (mask[0, col_index, p] > 0), 1.0, 0.0)
            column = jnp.sum(diagonal(p), axis=1, keepdims=True)
            value = out[0, p * BLOCK : (p + 1) * BLOCK, :]
            value = value - keep * column * weight[p * BLOCK : (p + 1) * BLOCK, :]
            above = row_id + p * BLOCK < col_id + col_index * PW
            out[0, p * BLOCK : (p + 1) * BLOCK, :] = jnp.where(is_panel & above, 0.0, value)

    for p in range(row_blocks):

        @pl.when(jnp.logical_not(is_panel) & (me * row_blocks + p == col_index))
        def _():
            out[0, p * BLOCK : (p + 1) * BLOCK, :] += diagonal(p)


def body(kids, maps, mask, diag):
    fronts, n_row, n_col = (lax.axis_size(name) for name in ("front", "row", "col"))
    chips = n_row // 2
    rows_dev = diag.shape[1]
    row_blocks = rows_dev // BLOCK
    rows_here = kids.shape[2]
    vmem, smem = pl.BlockSpec(memory_space=pltpu.VMEM), pl.BlockSpec(memory_space=pltpu.SMEM)
    anywhere = pl.BlockSpec(memory_space=pl.ANY)

    def along(x, by):
        return lax.ppermute(x, "row", [(i, (i + 2 * by) % n_row) for i in range(n_row)])

    def partner(x):
        return lax.ppermute(x, "row", [(i, i ^ 1) for i in range(n_row)])

    def parent(x, by):
        pairs = []
        for f in range(fronts):
            for i in range(n_row):
                pairs.append((f * n_row + i, (f - 1) % fronts * n_row + (i + 2 * by) % n_row))
        return lax.ppermute(x, ("front", "row"), pairs)

    def neighbour(x):
        return lax.ppermute(x, "col", [(i, i ^ 1) for i in range(n_col)])

    lines = WINDOW
    maps = jnp.swapaxes(maps, 2, 3)
    mask = jnp.swapaxes(mask, 1, 2)
    def shapes(*sizes):
        return [jax.ShapeDtypeStruct((size, BLOCK), BF16) for size in sizes]

    def both(x):
        return x, partner(x)

    hbm = pl.BlockSpec(memory_space=pltpu.HBM)
    kids = pltpu.with_memory_space_constraint(kids, pltpu.HBM)
    diag_hbm = pltpu.with_memory_space_constraint(diag, pltpu.HBM)
    tables, own_side, far_window, far_side = pl.pallas_call(
        select_kernel,
        out_shape=[jax.ShapeDtypeStruct((2, maps.shape[3]), jnp.int32)]
        + shapes(lines + 2 * rows_here, lines, lines + 2 * rows_here),
        in_specs=[hbm] * 3,
        out_specs=[vmem] * 4,
        scratch_shapes=[
            pltpu.VMEM(maps.shape, jnp.int32),
            pltpu.VMEM(diag.shape, F32),
            pltpu.VMEM((2, BLOCK, BLOCK), BF16),
            pltpu.SemaphoreType.DMA((14,)),
        ],
        compiler_params=params(),
        cost_estimate=cost(0),
        name="select",
    )(pltpu.with_memory_space_constraint(maps, pltpu.HBM), diag_hbm, kids)
    far_all, own_rest = pl.pallas_call(
        remain_kernel,
        out_shape=shapes(3 * rows_here, rows_here),
        in_specs=[smem, hbm],
        out_specs=[vmem] * 2,
        scratch_shapes=[pltpu.SemaphoreType.DMA((7,))],
        compiler_params=params(),
        cost_estimate=cost(0),
        name="remain",
    )(tables, kids)

    far_windows = [parent(far_window, s) for s in range(1, chips)]
    own_sides = [along(own_side, s) for s in range(1, chips)]
    far_near = parent(far_side, 0)
    own_side, own_rest, far_all = lax.optimization_barrier((own_side, own_rest, far_all))
    own_pair, own_rest = both(own_side), both(own_rest)
    arrived = (far_windows, own_sides, far_near, own_pair, own_rest, far_all)
    arrived = lax.optimization_barrier(arrived)
    far_windows, own_sides, far_near, own_pair, own_rest, far_all = arrived
    far_windows = [both(x) for x in far_windows]
    own_sides = [own_pair] + [both(x) for x in own_sides]
    far_near = both(far_near)
    far_alls = [parent(far_all, s) for s in range(1, chips)]
    own_parts = [x for pair in own_sides for x in pair]
    far_parts = list(far_near) + [x for pair in far_windows for x in pair]
    middle = slice(lines, lines + rows_here)
    halves = [x[middle] for x, _ in own_sides[1:]] + [far_near[0][middle]]
    others = neighbour(jnp.concatenate(halves, axis=0))
    far_table = far_near[0][NOTES + 7, : tables.shape[1]].astype(jnp.int32)
    square = jax.ShapeDtypeStruct((BLOCK, BLOCK), F32)
    first = pl.pallas_call(
        functools.partial(first_kernel, len(own_parts)),
        out_shape=[square] * 3,
        compiler_params=params(),
        cost_estimate=cost(0),
        name="first_factor",
    )(*own_parts, *far_parts)
    inverse = pl.pallas_call(
        second_kernel,
        out_shape=jax.ShapeDtypeStruct((NPANEL * PW, NPANEL * PW), F32),
        compiler_params=params(),
        cost_estimate=cost(0),
        name="second_factor",
    )(*first)

    remote, inverse = lax.optimization_barrier(((others, far_alls), inverse))
    others, far_alls = remote
    others = both(others)

    def owner(side, s):
        def position(me):
            core = me + 1 - 2 * (me % 2) if side else me
            return (core + n_row - 2 * s) % n_row

        return position

    layout, arrays = [], list(others)

    def add(child, s, first, second):
        for core in range(2):
            if isinstance(second, int):
                rest = (core, second * rows_here)
            else:
                rest = (len(arrays) + 1, 0) if second else (len(arrays), rows_here)
            start = lines if second is not None else 0
            column = start + rows_here if second is not None else 2 * rows_here
            layout.append((child, owner(core, s), (len(arrays), start), rest, column))
            arrays.append(first[core])
            if isinstance(second, tuple):
                arrays.append(second[core])

    far_alls = [both(x) for x in far_alls]
    add(0, 0, own_sides[0], own_rest)
    add(1, 0, far_near, chips - 1)
    for s in range(1, chips):
        add(0, s, own_sides[s], s - 1)
        add(1, s, far_alls[s - 1], None)

    tables = jnp.stack([tables[0], far_table])
    height = n_row * rows_here + BLOCK
    return pl.pallas_call(
        functools.partial(front_kernel, layout, n_row, row_blocks),
        out_shape=jax.ShapeDtypeStruct((1, rows_dev, PW), F32),
        in_specs=[smem, smem] + [vmem] * (2 + len(arrays)),
        out_specs=vmem,
        scratch_shapes=[
            pltpu.VMEM((NPANEL * PW, PW), F32),
            pltpu.VMEM((2, height, PW), F32),
            pltpu.VMEM((2, height, PW), BF16),
        ],
        compiler_params=params(),
        cost_estimate=cost(0),
        name="front",
    )(tables, mask, diag, inverse, *arrays)


def solution(mesh):
    in_specs = (
        P("front", None, "row", None),
        P("front", None, None, None),
        P("front", None, None),
        P("front", "row"),
    )
    out_specs = P("front", "row", "col")
    return jax.shard_map(body, mesh=mesh, in_specs=in_specs, out_specs=out_specs, check_vma=False)
```

```python
import functools

import jax
import jax.numpy as jnp
from jax import lax
from jax.experimental import pallas as pl
from jax.experimental.pallas import tpu as pltpu
from jax.sharding import PartitionSpec as P

BLOCK = 128
PW = 128
NPANEL = 2
F32 = jnp.float32
BF16 = jnp.bfloat16
HIGHEST = lax.Precision.HIGHEST
NOTES = 2 * BLOCK
WINDOW = NOTES + 16
MIB = 1024 * 1024


def params(mib=40):
    return pltpu.CompilerParams(vmem_limit_bytes=mib * MIB)


def copy_columns(kids, sems, copies, found, child, p, start, size, target, here=None):
    none = kids.shape[3] // BLOCK
    col = found[child][p]
    here = (col < none) if here is None else here & (col < none)
    start = pl.multiple_of(jnp.where(here, start, 0), 16)
    col = pl.multiple_of(jnp.where(here, col, 0) * BLOCK, BLOCK)
    source = kids.at[0, child, pl.ds(start, size), pl.ds(col, BLOCK)]
    copy = pltpu.make_async_copy(source, target, sems.at[len(copies)])
    copies.append((here, copy))

    @pl.when(here)
    def _():
        copy.start()

    @pl.when(jnp.logical_not(here))
    def _():
        target[...] = jnp.zeros_like(target)


def finish(copies):
    for here, copy in copies:

        @pl.when(here)
        def _():
            copy.wait()


def select_kernel(maps_hbm, diag_hbm, kids, tables, own_side, far_window, far_side, maps, diag, corner, sems):
    first = pltpu.make_async_copy(maps_hbm, maps, sems.at[sems.shape[0] - 2])
    second = pltpu.make_async_copy(diag_hbm, diag, sems.at[sems.shape[0] - 1])
    first.start()
    second.start()
    me, col_index = lax.axis_index("row"), lax.axis_index("col")
    rows = kids.shape[2]
    local = rows // BLOCK
    none = kids.shape[3] // BLOCK
    lines = far_window.shape[0]
    places = maps.shape[3]
    child_id = lax.broadcasted_iota(jnp.int32, (none, places), 0)
    place_id = lax.broadcasted_iota(jnp.int32, (1, places), 1)
    found = []
    first.wait()
    for child in range(2):
        ones = maps[0, child].astype(F32)
        line = jnp.sum(ones * (child_id - none).astype(F32), axis=0, keepdims=True) + none
        tables[child : child + 1, :] = line.astype(jnp.int32)
        found.append(
            [
                jnp.sum(jnp.where(place_id == w, line, 0.0)).astype(jnp.int32)
                for w in (0, 1, col_index)
            ]
        )
        if child == 1:
            line = jnp.broadcast_to(line, (16, places)).astype(BF16)
            table = jnp.concatenate([line, jnp.zeros((16, BLOCK - places), BF16)], axis=1)
    copies = []
    for child, out in ((0, own_side), (1, far_side)):
        targets = (out.at[pl.ds(0, BLOCK)], out.at[pl.ds(BLOCK, BLOCK)], corner.at[child])
        for (w, p), target in zip(((0, 0), (1, 0), (1, 1)), targets):
            row = found[child][w]
            offset = row - me * local
            here = (row < none) & (offset >= 0) & (offset < local)
            copy_columns(kids, sems, copies, found, child, p, offset * BLOCK, BLOCK, target, here)
    corners = list(copies)
    half = rows // 2
    for child, out in ((0, own_side), (1, far_side)):
        for p in range(NPANEL):
            target = out.at[pl.ds(lines + p * half, half)]
            copy_columns(kids, sems, copies, found, child, p, col_index % 2 * half, half, target)
        target = out.at[pl.ds(lines + rows, rows)]
        copy_columns(kids, sems, copies, found, child, NPANEL, 0, rows, target)

    second.wait()
    line = lax.broadcasted_iota(jnp.int32, (16, BLOCK), 0)
    pieces = jnp.zeros((16, BLOCK), F32)
    for p in range(NPANEL):
        rest = jnp.broadcast_to(diag[0:1, p * PW : (p + 1) * PW], (16, BLOCK))
        for at in range(3):
            part = rest.astype(BF16).astype(F32)
            pieces = jnp.where(line == 3 * p + at, part, pieces)
            rest = rest - part
    pieces = jnp.where(me == 0, pieces, 0.0)
    finish(corners)
    row_id = lax.broadcasted_iota(jnp.int32, (BLOCK, BLOCK), 0)
    col_id = lax.broadcasted_iota(jnp.int32, (BLOCK, BLOCK), 1)
    for child, out in ((0, own_side), (1, far_side)):
        upper = corner[child].astype(F32)
        lower = out[0:BLOCK, :].astype(F32)
        out[0:BLOCK, :] = jnp.where(row_id >= col_id, lower, upper).astype(BF16)
        middle = jnp.sum(jnp.where(row_id == col_id, upper, 0.0), axis=0, keepdims=True)
        notes = jnp.where(line == 6, jnp.broadcast_to(middle, (16, BLOCK)), 0.0)
        notes = notes + pieces if child == 0 else jnp.where(line == 7, table.astype(F32), notes)
        out[NOTES:lines, :] = notes.astype(BF16)
    far_window[...] = far_side[0:lines, :]
    finish(copies[len(corners) :])


def remain_kernel(tables, kids, far_all, own_rest, sems):
    col_index = lax.axis_index("col")
    rows = kids.shape[2]
    half = rows // 2
    here, other = col_index % 2 * half, (1 - col_index % 2) * half
    found = [[tables[child, w] for w in (0, 1, col_index)] for child in range(2)]
    copies = []
    for child, out, parts in (
        (
            1,
            far_all,
            [(0, here, half), (1, here, half), (0, other, half), (1, other, half), (2, 0, rows)],
        ),
        (0, own_rest, [(0, other, half), (1, other, half)]),
    ):
        at = 0
        for p, start, size in parts:
            target = out.at[pl.ds(at, size)]
            copy_columns(kids, sems, copies, found, child, p, start, size, target)
            at += size
    finish(copies)


def cost(microseconds):
    return pl.CostEstimate(flops=microseconds * 10**9, bytes_accessed=0, transcendentals=0)


def inverse_factor(tiles):
    tiles = list(tiles)
    count = len(tiles)
    lane = lax.broadcasted_iota(jnp.int32, (8, BLOCK), 1)
    line = lax.broadcasted_iota(jnp.int32, (8, BLOCK), 0)
    wide = lambda x: jnp.broadcast_to(x, (8, BLOCK))
    result = []
    for b in range(count):
        low = 8 * b
        tile = tiles[b]
        columns = [wide(tile[:, low + j : low + j + 1]) for j in range(8)]
        d = [[wide(columns[j][i : i + 1, :]) if i >= j else None for j in range(8)] for i in range(8)]
        inside = (lane >= low) & (lane < low + 8)
        rows = [
            jnp.where(inside, (lane == low + i).astype(F32), wide(tile[i : i + 1, :]))
            for i in range(8)
        ]
        scale = []
        for j in range(8):
            scale.append(lax.rsqrt(d[j][j]))
            for i in range(j + 1, 8):
                d[i][j] = d[i][j] * scale[j]
            for k in range(j + 1, 8):
                for i in range(k, 8):
                    d[i][k] = d[i][k] - d[i][j] * d[k][j]
            rows[j] = rows[j] * scale[j]
            for i in range(j + 1, 8):
                rows[i] = rows[i] - d[i][j] * rows[j]
        merged = rows[0]
        for j in range(1, 8):
            merged = jnp.where(line == j, rows[j], merged)
        result.append(jnp.where(lane < low + 8, merged, 0.0))
        for t in range(b + 1, count):
            tile = tiles[t]
            columns = [wide(tile[:, low + j : low + j + 1]) for j in range(8)]
            tile = jnp.where(inside, 0.0, tile)
            for j in range(8):
                for m in range(j):
                    columns[j] = columns[j] - columns[m] * d[j][m]
                columns[j] = columns[j] * scale[j]
                tile = tile - columns[j] * rows[j]
            tiles[t] = tile
    return result


def dot(a, b, lhs=1, rhs=0):
    return lax.dot_general(
        a, b, (((lhs,), (rhs,)), ((), ())), precision=HIGHEST, preferred_element_type=F32
    )


def invert(block):
    tiles = [block[8 * t : 8 * t + 8, :] for t in range(BLOCK // 8)]
    return jnp.concatenate(inverse_factor(tiles), axis=0)


def factor_kernel(n_own, *refs):
    own, far = refs[:n_own], refs[n_own:-2]
    whole, panel = refs[-2:]

    def total(group, start, size):
        value = None
        for ref in group:
            part = ref[start : start + size, :].astype(F32)
            value = part if value is None else value + part
        return value

    row_id = lax.broadcasted_iota(jnp.int32, (BLOCK, BLOCK), 0)
    col_id = lax.broadcasted_iota(jnp.int32, (BLOCK, BLOCK), 1)
    own_notes, far_notes = total(own, NOTES, 16), total(far, NOTES, 16)

    def diagonal(line):
        return jnp.where(row_id == col_id, jnp.broadcast_to(line, (BLOCK, BLOCK)), 0.0)

    def initial(p):
        line = own_notes[3 * p : 3 * p + 1] + own_notes[3 * p + 1 : 3 * p + 2]
        return line + own_notes[3 * p + 2 : 3 * p + 3]

    corners = total(own + far, 0, BLOCK)
    lower = jnp.where(row_id > col_id, corners, 0.0)
    middle = jnp.where(row_id == col_id, corners, 0.0)
    upper = jnp.where(row_id < col_id, corners, 0.0)
    first = invert(lower + lower.T + middle + diagonal(initial(0)))
    below = dot(total(own + far, BLOCK, BLOCK), first, 1, 1)
    line = own_notes[6:7] + far_notes[6:7] + initial(1)
    inverse = invert(upper + upper.T + diagonal(line) - dot(below, below, 1, 1))
    base = dot(first, first, 0, 0)
    corner = -dot(inverse, dot(below, first))
    side = dot(corner, inverse, 0, 0)
    left = jnp.concatenate([base + dot(corner, corner, 0, 0), side.T], axis=0)
    right = jnp.concatenate([side, dot(inverse, inverse, 0, 0)], axis=0)
    rest = jnp.concatenate([left, right], axis=1)
    for at in range(3):
        whole[at] = rest.astype(BF16)
        rest = rest - whole[at].astype(F32)
    is_first = lax.axis_index("col") == 0
    panel[0:BLOCK, :] = -jnp.where(is_first, first, corner).T
    panel[BLOCK:, :] = -jnp.where(is_first, 0.0, inverse.T)


def front_kernel(layout, n_row, row_blocks, tables, mask, diag, whole, panel, *refs):
    out, weight, product, buffer = refs[-4:]
    me, col_index = lax.axis_index("row"), lax.axis_index("col")
    is_panel = col_index < NPANEL
    rows = (product.shape[1] - BLOCK) // n_row
    half = rows // 2
    wide = NPANEL * PW
    parts = []
    for child, owner, (first, start), (second, at), column in layout:
        parts.append((child, owner(me), refs[first], start, col_index % 2))
        parts.append((child, owner(me), refs[second], at, 1 - col_index % 2))
        start = pl.multiple_of(owner(me) * rows, rows)
        buffer[child, pl.ds(start, rows), :] = refs[first][column : column + rows, :]

    mirrored = [jnp.zeros((BLOCK, wide), F32)] * 2
    for child, owner, ref, at, side in parts:
        index = tables[child, col_index] * BLOCK
        for step in range(0, BLOCK, BLOCK // 2):
            place = index + step - owner * rows - side * half
            inside = (place >= 0) & (place < half)
            place = pl.multiple_of(jnp.where(inside, place, 0), BLOCK // 2)
            lines = [ref[pl.ds(at + p * half + place, BLOCK // 2), :] for p in range(NPANEL)]
            lines = jnp.where(inside, jnp.concatenate(lines, axis=1).astype(F32), 0.0)
            empty = jnp.zeros_like(lines)
            lines = [lines, empty] if step == 0 else [empty, lines]
            mirrored[child] = mirrored[child] + jnp.concatenate(lines, axis=0)

    solved = panel[...] * jnp.where(is_panel, 1.0, 0.0)
    keep = jnp.where(is_panel, 0.0, 1.0)
    for lines in mirrored:
        lines = (lines * keep).astype(BF16)
        for at in range(3):
            solved = solved + lax.dot_general(
                whole[at], lines, (((1,), (1,)), ((), ())), preferred_element_type=F32
            )
    weight[...] = solved
    high = weight[...].astype(BF16)
    low = (weight[...] - high.astype(F32)).astype(BF16)
    both = jnp.concatenate([high, low], axis=1)
    for child, owner, ref, at, side in parts:
        left = jnp.concatenate(
            [ref[at + p * half : at + (p + 1) * half, :] for p in range(NPANEL)], axis=1
        )
        value = jnp.dot(left, both, preferred_element_type=F32)
        start = pl.multiple_of(owner * rows + side * half, half)
        product[child, pl.ds(start, half), :] = value[:, :PW] + value[:, PW:]
    for child in range(2):
        product[child, n_row * rows :, :] = jnp.zeros((BLOCK, PW), F32)
        buffer[child, n_row * rows :, :] = jnp.zeros((BLOCK, PW), BF16)

    for p in range(row_blocks):
        at = me * row_blocks + p
        first, second = (
            pl.ds(pl.multiple_of(tables[child, at] * BLOCK, BLOCK), BLOCK) for child in range(2)
        )
        base = buffer[0, first, :].astype(F32) + buffer[1, second, :].astype(F32)
        keep = jnp.where(is_panel | (mask[0, col_index, at] > 0), 1.0, 0.0)
        value = jnp.where(is_panel, 0.0, base) - keep * (product[0, first, :] + product[1, second, :])
        out[0, p * BLOCK : (p + 1) * BLOCK, :] = value

    row_id = lax.broadcasted_iota(jnp.int32, (BLOCK, BLOCK), 0)
    col_id = lax.broadcasted_iota(jnp.int32, (BLOCK, BLOCK), 1)

    def diagonal(p):
        line = jnp.broadcast_to(diag[0:1, p * BLOCK : (p + 1) * BLOCK], (BLOCK, BLOCK))
        return jnp.where(row_id == col_id, line, 0.0)

    for p in range(NPANEL):

        @pl.when(me == 0)
        def _():
            keep = jnp.where(is_panel | (mask[0, col_index, p] > 0), 1.0, 0.0)
            column = jnp.sum(diagonal(p), axis=1, keepdims=True)
            value = out[0, p * BLOCK : (p + 1) * BLOCK, :]
            value = value - keep * column * weight[p * BLOCK : (p + 1) * BLOCK, :]
            above = row_id + p * BLOCK < col_id + col_index * PW
            out[0, p * BLOCK : (p + 1) * BLOCK, :] = jnp.where(is_panel & above, 0.0, value)

    for p in range(row_blocks):

        @pl.when(jnp.logical_not(is_panel) & (me * row_blocks + p == col_index))
        def _():
            out[0, p * BLOCK : (p + 1) * BLOCK, :] += diagonal(p)


def body(kids, maps, mask, diag):
    fronts, n_row, n_col = (lax.axis_size(name) for name in ("front", "row", "col"))
    chips = n_row // 2
    rows_dev = diag.shape[1]
    row_blocks = rows_dev // BLOCK
    rows_here = kids.shape[2]
    vmem, smem = pl.BlockSpec(memory_space=pltpu.VMEM), pl.BlockSpec(memory_space=pltpu.SMEM)
    anywhere = pl.BlockSpec(memory_space=pl.ANY)

    def along(x, by):
        return lax.ppermute(x, "row", [(i, (i + 2 * by) % n_row) for i in range(n_row)])

    def partner(x):
        return lax.ppermute(x, "row", [(i, i ^ 1) for i in range(n_row)])

    def parent(x, by):
        pairs = []
        for f in range(fronts):
            for i in range(n_row):
                pairs.append((f * n_row + i, (f - 1) % fronts * n_row + (i + 2 * by) % n_row))
        return lax.ppermute(x, ("front", "row"), pairs)

    def neighbour(x):
        return lax.ppermute(x, "col", [(i, i ^ 1) for i in range(n_col)])

    lines = WINDOW
    maps = jnp.swapaxes(maps, 2, 3)
    mask = jnp.swapaxes(mask, 1, 2)
    def shapes(*sizes):
        return [jax.ShapeDtypeStruct((size, BLOCK), BF16) for size in sizes]

    def both(x):
        return x, partner(x)

    hbm = pl.BlockSpec(memory_space=pltpu.HBM)
    kids = pltpu.with_memory_space_constraint(kids, pltpu.HBM)
    diag_hbm = pltpu.with_memory_space_constraint(diag, pltpu.HBM)
    tables, own_side, far_window, far_side = pl.pallas_call(
        select_kernel,
        out_shape=[jax.ShapeDtypeStruct((2, maps.shape[3]), jnp.int32)]
        + shapes(lines + 2 * rows_here, lines, lines + 2 * rows_here),
        in_specs=[hbm] * 3,
        out_specs=[vmem] * 4,
        scratch_shapes=[
            pltpu.VMEM(maps.shape, jnp.int32),
            pltpu.VMEM(diag.shape, F32),
            pltpu.VMEM((2, BLOCK, BLOCK), BF16),
            pltpu.SemaphoreType.DMA((14,)),
        ],
        compiler_params=params(),
        cost_estimate=cost(0),
        name="select",
    )(pltpu.with_memory_space_constraint(maps, pltpu.HBM), diag_hbm, kids)
    far_all, own_rest = pl.pallas_call(
        remain_kernel,
        out_shape=shapes(3 * rows_here, rows_here),
        in_specs=[smem, hbm],
        out_specs=[vmem] * 2,
        scratch_shapes=[pltpu.SemaphoreType.DMA((7,))],
        compiler_params=params(),
        cost_estimate=cost(0),
        name="remain",
    )(tables, kids)

    far_windows = [parent(far_window, s) for s in range(1, chips)]
    own_sides = [along(own_side, s) for s in range(1, chips)]
    far_near = parent(far_side, 0)
    own_side, own_rest, far_all = lax.optimization_barrier((own_side, own_rest, far_all))
    own_pair, own_rest = both(own_side), both(own_rest)
    own_sides, far_all = lax.optimization_barrier((own_sides, far_all))
    far_alls = [parent(far_all, s) for s in range(1, chips)]
    arrived = (far_windows, own_sides, far_near, own_pair, own_rest)
    far_windows, own_sides, far_near, own_pair, own_rest = lax.optimization_barrier(arrived)
    far_windows = [both(x) for x in far_windows]
    own_sides = [own_pair] + [both(x) for x in own_sides]
    far_near = both(far_near)
    own_parts = [x for pair in own_sides for x in pair]
    far_parts = list(far_near) + [x for pair in far_windows for x in pair]
    middle = slice(lines, lines + rows_here)
    halves = [x[middle] for x, _ in own_sides[1:]] + [far_near[0][middle]]
    others = neighbour(jnp.concatenate(halves, axis=0))
    far_table = far_near[0][NOTES + 7, : tables.shape[1]].astype(jnp.int32)
    factors = pl.pallas_call(
        functools.partial(factor_kernel, len(own_parts)),
        out_shape=[
            jax.ShapeDtypeStruct((3, NPANEL * PW, NPANEL * PW), BF16),
            jax.ShapeDtypeStruct((NPANEL * PW, PW), F32),
        ],
        compiler_params=params(),
        cost_estimate=cost(0),
        name="factor",
    )(*own_parts, *far_parts)

    remote, factors = lax.optimization_barrier(((others, far_alls), factors))
    others, far_alls = remote
    others = both(others)

    def owner(side, s):
        def position(me):
            core = me + 1 - 2 * (me % 2) if side else me
            return (core + n_row - 2 * s) % n_row

        return position

    layout, arrays = [], list(others)

    def add(child, s, first, second):
        for core in range(2):
            if isinstance(second, int):
                rest = (core, second * rows_here)
            else:
                rest = (len(arrays) + 1, 0) if second else (len(arrays), rows_here)
            start = lines if second is not None else 0
            column = start + rows_here if second is not None else 2 * rows_here
            layout.append((child, owner(core, s), (len(arrays), start), rest, column))
            arrays.append(first[core])
            if isinstance(second, tuple):
                arrays.append(second[core])

    far_alls = [both(x) for x in far_alls]
    add(0, 0, own_sides[0], own_rest)
    add(1, 0, far_near, chips - 1)
    for s in range(1, chips):
        add(0, s, own_sides[s], s - 1)
        add(1, s, far_alls[s - 1], None)

    tables = jnp.stack([tables[0], far_table])
    height = n_row * rows_here + BLOCK
    return pl.pallas_call(
        functools.partial(front_kernel, layout, n_row, row_blocks),
        out_shape=jax.ShapeDtypeStruct((1, rows_dev, PW), F32),
        in_specs=[smem, smem] + [vmem] * (3 + len(arrays)),
        out_specs=vmem,
        scratch_shapes=[
            pltpu.VMEM((NPANEL * PW, PW), F32),
            pltpu.VMEM((2, height, PW), F32),
            pltpu.VMEM((2, height, PW), BF16),
        ],
        compiler_params=params(),
        cost_estimate=cost(0),
        name="front",
    )(tables, mask, diag, *factors, *arrays)


def solution(mesh):
    in_specs = (
        P("front", None, "row", None),
        P("front", None, None, None),
        P("front", None, None),
        P("front", "row"),
    )
    out_specs = P("front", "row", "col")
    return jax.shard_map(body, mesh=mesh, in_specs=in_specs, out_specs=out_specs, check_vma=False)
```

```python
import functools

import jax
import jax.numpy as jnp
from jax import lax
from jax.experimental import pallas as pl
from jax.experimental.pallas import tpu as pltpu
from jax.sharding import PartitionSpec as P

BLOCK = 128
PW = 128
NPANEL = 2
F32 = jnp.float32
BF16 = jnp.bfloat16
HIGHEST = lax.Precision.HIGHEST
NOTES = 2 * BLOCK
WINDOW = NOTES + 16
MIB = 1024 * 1024


def params(mib=40):
    return pltpu.CompilerParams(vmem_limit_bytes=mib * MIB)


def copy_columns(kids, sems, copies, found, child, p, start, size, target, here=None):
    none = kids.shape[3] // BLOCK
    col = found[child][p]
    here = (col < none) if here is None else here & (col < none)
    start = pl.multiple_of(jnp.where(here, start, 0), 16)
    col = pl.multiple_of(jnp.where(here, col, 0) * BLOCK, BLOCK)
    source = kids.at[0, child, pl.ds(start, size), pl.ds(col, BLOCK)]
    copy = pltpu.make_async_copy(source, target, sems.at[len(copies)])
    copies.append((here, copy))

    @pl.when(here)
    def _():
        copy.start()

    @pl.when(jnp.logical_not(here))
    def _():
        target[...] = jnp.zeros_like(target)


def finish(copies):
    for here, copy in copies:

        @pl.when(here)
        def _():
            copy.wait()


def select_kernel(maps_hbm, diag_hbm, kids, tables, own_side, far_window, far_side, maps, diag, corner, sems):
    first = pltpu.make_async_copy(maps_hbm, maps, sems.at[sems.shape[0] - 2])
    second = pltpu.make_async_copy(diag_hbm, diag, sems.at[sems.shape[0] - 1])
    first.start()
    second.start()
    me, col_index = lax.axis_index("row"), lax.axis_index("col")
    rows = kids.shape[2]
    local = rows // BLOCK
    none = kids.shape[3] // BLOCK
    lines = far_window.shape[0]
    places = maps.shape[3]
    child_id = lax.broadcasted_iota(jnp.int32, (none, places), 0)
    place_id = lax.broadcasted_iota(jnp.int32, (1, places), 1)
    found = []
    first.wait()
    for child in range(2):
        ones = maps[0, child].astype(F32)
        line = jnp.sum(ones * (child_id - none).astype(F32), axis=0, keepdims=True) + none
        tables[child : child + 1, :] = line.astype(jnp.int32)
        found.append(
            [
                jnp.sum(jnp.where(place_id == w, line, 0.0)).astype(jnp.int32)
                for w in (0, 1, col_index)
            ]
        )
        if child == 1:
            line = jnp.broadcast_to(line, (16, places)).astype(BF16)
            table = jnp.concatenate([line, jnp.zeros((16, BLOCK - places), BF16)], axis=1)
    copies = []
    for child, out in ((0, own_side), (1, far_side)):
        targets = (out.at[pl.ds(0, BLOCK)], out.at[pl.ds(BLOCK, BLOCK)], corner.at[child])
        for (w, p), target in zip(((0, 0), (1, 0), (1, 1)), targets):
            row = found[child][w]
            offset = row - me * local
            here = (row < none) & (offset >= 0) & (offset < local)
            copy_columns(kids, sems, copies, found, child, p, offset * BLOCK, BLOCK, target, here)
    corners = list(copies)
    half = rows // 2
    for child, out in ((0, own_side), (1, far_side)):
        for p in range(NPANEL):
            target = out.at[pl.ds(lines + p * half, half)]
            copy_columns(kids, sems, copies, found, child, p, col_index % 2 * half, half, target)
        target = out.at[pl.ds(lines + rows, rows)]
        copy_columns(kids, sems, copies, found, child, NPANEL, 0, rows, target)

    second.wait()
    line = lax.broadcasted_iota(jnp.int32, (16, BLOCK), 0)
    pieces = jnp.zeros((16, BLOCK), F32)
    for p in range(NPANEL):
        rest = jnp.broadcast_to(diag[0:1, p * PW : (p + 1) * PW], (16, BLOCK))
        for at in range(3):
            part = rest.astype(BF16).astype(F32)
            pieces = jnp.where(line == 3 * p + at, part, pieces)
            rest = rest - part
    pieces = jnp.where(me == 0, pieces, 0.0)
    finish(corners)
    row_id = lax.broadcasted_iota(jnp.int32, (BLOCK, BLOCK), 0)
    col_id = lax.broadcasted_iota(jnp.int32, (BLOCK, BLOCK), 1)
    for child, out in ((0, own_side), (1, far_side)):
        upper = corner[child].astype(F32)
        lower = out[0:BLOCK, :].astype(F32)
        out[0:BLOCK, :] = jnp.where(row_id >= col_id, lower, upper).astype(BF16)
        middle = jnp.sum(jnp.where(row_id == col_id, upper, 0.0), axis=0, keepdims=True)
        notes = jnp.where(line == 6, jnp.broadcast_to(middle, (16, BLOCK)), 0.0)
        notes = notes + pieces if child == 0 else jnp.where(line == 7, table.astype(F32), notes)
        out[NOTES:lines, :] = notes.astype(BF16)
    far_window[...] = far_side[0:lines, :]
    finish(copies[len(corners) :])


def remain_kernel(tables, kids, far_all, own_rest, sems):
    col_index = lax.axis_index("col")
    rows = kids.shape[2]
    half = rows // 2
    here, other = col_index % 2 * half, (1 - col_index % 2) * half
    found = [[tables[child, w] for w in (0, 1, col_index)] for child in range(2)]
    copies = []
    for child, out, parts in (
        (
            1,
            far_all,
            [(0, here, half), (1, here, half), (0, other, half), (1, other, half), (2, 0, rows)],
        ),
        (0, own_rest, [(0, other, half), (1, other, half)]),
    ):
        at = 0
        for p, start, size in parts:
            target = out.at[pl.ds(at, size)]
            copy_columns(kids, sems, copies, found, child, p, start, size, target)
            at += size
    finish(copies)


def cost(microseconds):
    return pl.CostEstimate(flops=microseconds * 10**9, bytes_accessed=0, transcendentals=0)


def inverse_factor(tiles):
    tiles = list(tiles)
    count = len(tiles)
    lane = lax.broadcasted_iota(jnp.int32, (8, BLOCK), 1)
    line = lax.broadcasted_iota(jnp.int32, (8, BLOCK), 0)
    wide = lambda x: jnp.broadcast_to(x, (8, BLOCK))
    result = []
    for b in range(count):
        low = 8 * b
        tile = tiles[b]
        columns = [wide(tile[:, low + j : low + j + 1]) for j in range(8)]
        d = [[wide(columns[j][i : i + 1, :]) if i >= j else None for j in range(8)] for i in range(8)]
        inside = (lane >= low) & (lane < low + 8)
        rows = [
            jnp.where(inside, (lane == low + i).astype(F32), wide(tile[i : i + 1, :]))
            for i in range(8)
        ]
        scale = []
        for j in range(8):
            scale.append(lax.rsqrt(d[j][j]))
            for i in range(j + 1, 8):
                d[i][j] = d[i][j] * scale[j]
            for k in range(j + 1, 8):
                for i in range(k, 8):
                    d[i][k] = d[i][k] - d[i][j] * d[k][j]
            rows[j] = rows[j] * scale[j]
            for i in range(j + 1, 8):
                rows[i] = rows[i] - d[i][j] * rows[j]
        merged = rows[0]
        for j in range(1, 8):
            merged = jnp.where(line == j, rows[j], merged)
        result.append(jnp.where(lane < low + 8, merged, 0.0))
        for t in range(b + 1, count):
            tile = tiles[t]
            columns = [wide(tile[:, low + j : low + j + 1]) for j in range(8)]
            tile = jnp.where(inside, 0.0, tile)
            for j in range(8):
                for m in range(j):
                    columns[j] = columns[j] - columns[m] * d[j][m]
                columns[j] = columns[j] * scale[j]
                tile = tile - columns[j] * rows[j]
            tiles[t] = tile
    return result


def dot(a, b, lhs=1, rhs=0):
    return lax.dot_general(
        a, b, (((lhs,), (rhs,)), ((), ())), precision=HIGHEST, preferred_element_type=F32
    )


def invert(block):
    tiles = [block[8 * t : 8 * t + 8, :] for t in range(BLOCK // 8)]
    return jnp.concatenate(inverse_factor(tiles), axis=0)


def factor_kernel(n_own, *refs):
    own, far = refs[:n_own], refs[n_own:-2]
    whole, panel = refs[-2:]

    def total(group, start, size):
        value = None
        for ref in group:
            part = ref[start : start + size, :].astype(F32)
            value = part if value is None else value + part
        return value

    row_id = lax.broadcasted_iota(jnp.int32, (BLOCK, BLOCK), 0)
    col_id = lax.broadcasted_iota(jnp.int32, (BLOCK, BLOCK), 1)
    own_notes, far_notes = total(own, NOTES, 16), total(far, NOTES, 16)

    def diagonal(line):
        return jnp.where(row_id == col_id, jnp.broadcast_to(line, (BLOCK, BLOCK)), 0.0)

    def initial(p):
        line = own_notes[3 * p : 3 * p + 1] + own_notes[3 * p + 1 : 3 * p + 2]
        return line + own_notes[3 * p + 2 : 3 * p + 3]

    corners = total(own + far, 0, BLOCK)
    lower = jnp.where(row_id > col_id, corners, 0.0)
    middle = jnp.where(row_id == col_id, corners, 0.0)
    upper = jnp.where(row_id < col_id, corners, 0.0)
    first = invert(lower + lower.T + middle + diagonal(initial(0)))
    below = dot(total(own + far, BLOCK, BLOCK), first, 1, 1)
    line = own_notes[6:7] + far_notes[6:7] + initial(1)
    inverse = invert(upper + upper.T + diagonal(line) - dot(below, below, 1, 1))
    base = dot(first, first, 0, 0)
    corner = -dot(inverse, dot(below, first))
    side = dot(corner, inverse, 0, 0)
    left = jnp.concatenate([base + dot(corner, corner, 0, 0), side.T], axis=0)
    right = jnp.concatenate([side, dot(inverse, inverse, 0, 0)], axis=0)
    rest = jnp.concatenate([left, right], axis=1)
    for at in range(3):
        whole[at] = rest.astype(BF16)
        rest = rest - whole[at].astype(F32)
    is_first = lax.axis_index("col") == 0
    panel[0:BLOCK, :] = -jnp.where(is_first, first, corner).T
    panel[BLOCK:, :] = -jnp.where(is_first, 0.0, inverse.T)


def front_kernel(layout, n_row, row_blocks, tables_any, mask_any, diag, whole, panel, *refs):
    result, out, weight, product, buffer, tables, mask, sems = refs[-8:]
    first_copy = pltpu.make_async_copy(tables_any, tables, sems.at[0])
    second_copy = pltpu.make_async_copy(mask_any, mask, sems.at[1])
    first_copy.start()
    second_copy.start()
    me, col_index = lax.axis_index("row"), lax.axis_index("col")
    is_panel = col_index < NPANEL
    rows = (product.shape[1] - BLOCK) // n_row
    half = rows // 2
    wide = NPANEL * PW
    parts = []
    for child, owner, (first, start), (second, at), column in layout:
        parts.append((child, owner(me), refs[first], start, col_index % 2))
        parts.append((child, owner(me), refs[second], at, 1 - col_index % 2))
        start = pl.multiple_of(owner(me) * rows, rows)
        buffer[child, pl.ds(start, rows), :] = refs[first][column : column + rows, :]

    for child in range(2):
        product[child, n_row * rows :, :] = jnp.zeros((BLOCK, PW), F32)
        buffer[child, n_row * rows :, :] = jnp.zeros((BLOCK, PW), BF16)
    first_copy.wait()
    second_copy.wait()

    mirrored = [jnp.zeros((BLOCK, wide), F32)] * 2
    for child, owner, ref, at, side in parts:
        index = tables[child, col_index] * BLOCK
        for step in range(0, BLOCK, BLOCK // 2):
            place = index + step - owner * rows - side * half
            inside = (place >= 0) & (place < half)
            place = pl.multiple_of(jnp.where(inside, place, 0), BLOCK // 2)
            lines = [ref[pl.ds(at + p * half + place, BLOCK // 2), :] for p in range(NPANEL)]
            lines = jnp.where(inside, jnp.concatenate(lines, axis=1).astype(F32), 0.0)
            empty = jnp.zeros_like(lines)
            lines = [lines, empty] if step == 0 else [empty, lines]
            mirrored[child] = mirrored[child] + jnp.concatenate(lines, axis=0)

    solved = panel[...] * jnp.where(is_panel, 1.0, 0.0)
    keep = jnp.where(is_panel, 0.0, 1.0)
    for lines in mirrored:
        lines = (lines * keep).astype(BF16)
        for at in range(3):
            solved = solved + lax.dot_general(
                whole[at], lines, (((1,), (1,)), ((), ())), preferred_element_type=F32
            )
    weight[...] = solved
    high = weight[...].astype(BF16)
    low = (weight[...] - high.astype(F32)).astype(BF16)
    both = jnp.concatenate([high, low], axis=1)
    for child, owner, ref, at, side in parts:
        left = jnp.concatenate(
            [ref[at + p * half : at + (p + 1) * half, :] for p in range(NPANEL)], axis=1
        )
        value = jnp.dot(left, both, preferred_element_type=F32)
        start = pl.multiple_of(owner * rows + side * half, half)
        product[child, pl.ds(start, half), :] = value[:, :PW] + value[:, PW:]
    row_id = lax.broadcasted_iota(jnp.int32, (BLOCK, BLOCK), 0)
    col_id = lax.broadcasted_iota(jnp.int32, (BLOCK, BLOCK), 1)

    def diagonal(p):
        line = jnp.broadcast_to(diag[0:1, p * BLOCK : (p + 1) * BLOCK], (BLOCK, BLOCK))
        return jnp.where(row_id == col_id, line, 0.0)

    def place(p):
        at = me * row_blocks + p
        first, second = (
            pl.ds(pl.multiple_of(tables[child, at] * BLOCK, BLOCK), BLOCK) for child in range(2)
        )
        base = buffer[0, first, :].astype(F32) + buffer[1, second, :].astype(F32)
        keep = jnp.where(is_panel | (mask[0, col_index, at] > 0), 1.0, 0.0)
        value = jnp.where(is_panel, 0.0, base) - keep * (product[0, first, :] + product[1, second, :])
        out[p * BLOCK : (p + 1) * BLOCK, :] = value

    def correct(p):
        @pl.when(me == 0)
        def _():
            keep = jnp.where(is_panel | (mask[0, col_index, p] > 0), 1.0, 0.0)
            column = jnp.sum(diagonal(p), axis=1, keepdims=True)
            value = out[p * BLOCK : (p + 1) * BLOCK, :]
            value = value - keep * column * weight[p * BLOCK : (p + 1) * BLOCK, :]
            above = row_id + p * BLOCK < col_id + col_index * PW
            out[p * BLOCK : (p + 1) * BLOCK, :] = jnp.where(is_panel & above, 0.0, value)

    def add_diagonal(p):
        @pl.when(jnp.logical_not(is_panel) & (me * row_blocks + p == col_index))
        def _():
            out[p * BLOCK : (p + 1) * BLOCK, :] += diagonal(p)

    copies = []
    step = 3
    for start in range(0, row_blocks, step):
        for p in range(start, start + step):
            place(p)
        for p in range(start, start + step):
            if p < NPANEL:
                correct(p)
            add_diagonal(p)
        lines = pl.ds(start * BLOCK, step * BLOCK)
        copy = pltpu.make_async_copy(out.at[lines], result.at[0, lines], sems.at[2 + start // step])
        copy.start()
        copies.append(copy)
    for copy in copies:
        copy.wait()


def body(kids, maps, mask, diag):
    fronts, n_row, n_col = (lax.axis_size(name) for name in ("front", "row", "col"))
    chips = n_row // 2
    rows_dev = diag.shape[1]
    row_blocks = rows_dev // BLOCK
    rows_here = kids.shape[2]
    vmem, smem = pl.BlockSpec(memory_space=pltpu.VMEM), pl.BlockSpec(memory_space=pltpu.SMEM)
    anywhere = pl.BlockSpec(memory_space=pl.ANY)

    def along(x, by):
        return lax.ppermute(x, "row", [(i, (i + 2 * by) % n_row) for i in range(n_row)])

    def partner(x):
        return lax.ppermute(x, "row", [(i, i ^ 1) for i in range(n_row)])

    def parent(x, by):
        pairs = []
        for f in range(fronts):
            for i in range(n_row):
                pairs.append((f * n_row + i, (f - 1) % fronts * n_row + (i + 2 * by) % n_row))
        return lax.ppermute(x, ("front", "row"), pairs)

    def neighbour(x):
        return lax.ppermute(x, "col", [(i, i ^ 1) for i in range(n_col)])

    lines = WINDOW
    maps = jnp.swapaxes(maps, 2, 3)
    mask = jnp.swapaxes(mask, 1, 2)
    def shapes(*sizes):
        return [jax.ShapeDtypeStruct((size, BLOCK), BF16) for size in sizes]

    def both(x):
        return x, partner(x)

    hbm = pl.BlockSpec(memory_space=pltpu.HBM)
    kids = pltpu.with_memory_space_constraint(kids, pltpu.HBM)
    diag_hbm = pltpu.with_memory_space_constraint(diag, pltpu.HBM)
    tables, own_side, far_window, far_side = pl.pallas_call(
        select_kernel,
        out_shape=[jax.ShapeDtypeStruct((2, maps.shape[3]), jnp.int32)]
        + shapes(lines + 2 * rows_here, lines, lines + 2 * rows_here),
        in_specs=[hbm] * 3,
        out_specs=[vmem] * 4,
        scratch_shapes=[
            pltpu.VMEM(maps.shape, jnp.int32),
            pltpu.VMEM(diag.shape, F32),
            pltpu.VMEM((2, BLOCK, BLOCK), BF16),
            pltpu.SemaphoreType.DMA((14,)),
        ],
        compiler_params=params(),
        cost_estimate=cost(0),
        name="select",
    )(pltpu.with_memory_space_constraint(maps, pltpu.HBM), diag_hbm, kids)
    far_all, own_rest = pl.pallas_call(
        remain_kernel,
        out_shape=shapes(3 * rows_here, rows_here),
        in_specs=[smem, hbm],
        out_specs=[vmem] * 2,
        scratch_shapes=[pltpu.SemaphoreType.DMA((7,))],
        compiler_params=params(),
        cost_estimate=cost(0),
        name="remain",
    )(tables, kids)

    far_windows = [parent(far_window, s) for s in range(1, chips)]
    own_sides = [along(own_side, s) for s in range(1, chips)]
    far_near = parent(far_side, 0)
    own_side, own_rest, far_all = lax.optimization_barrier((own_side, own_rest, far_all))
    own_pair, own_rest = both(own_side), both(own_rest)
    own_sides, far_all = lax.optimization_barrier((own_sides, far_all))
    far_alls = [parent(far_all, s) for s in range(1, chips)]
    arrived = (far_windows, own_sides, far_near, own_pair, own_rest)
    far_windows, own_sides, far_near, own_pair, own_rest = lax.optimization_barrier(arrived)
    far_windows = [both(x) for x in far_windows]
    own_sides = [own_pair] + [both(x) for x in own_sides]
    far_near = both(far_near)
    own_parts = [x for pair in own_sides for x in pair]
    far_parts = list(far_near) + [x for pair in far_windows for x in pair]
    middle = slice(lines, lines + rows_here)
    halves = [x[middle] for x, _ in own_sides[1:]] + [far_near[0][middle]]
    others = neighbour(jnp.concatenate(halves, axis=0))
    far_table = far_near[0][NOTES + 7, : tables.shape[1]].astype(jnp.int32)
    factors = pl.pallas_call(
        functools.partial(factor_kernel, len(own_parts)),
        out_shape=[
            jax.ShapeDtypeStruct((3, NPANEL * PW, NPANEL * PW), BF16),
            jax.ShapeDtypeStruct((NPANEL * PW, PW), F32),
        ],
        compiler_params=params(),
        cost_estimate=cost(0),
        name="factor",
    )(*own_parts, *far_parts)

    remote, factors = lax.optimization_barrier(((others, far_alls), factors))
    others, far_alls = remote
    others = both(others)

    def owner(side, s):
        def position(me):
            core = me + 1 - 2 * (me % 2) if side else me
            return (core + n_row - 2 * s) % n_row

        return position

    layout, arrays = [], list(others)

    def add(child, s, first, second):
        for core in range(2):
            if isinstance(second, int):
                rest = (core, second * rows_here)
            else:
                rest = (len(arrays) + 1, 0) if second else (len(arrays), rows_here)
            start = lines if second is not None else 0
            column = start + rows_here if second is not None else 2 * rows_here
            layout.append((child, owner(core, s), (len(arrays), start), rest, column))
            arrays.append(first[core])
            if isinstance(second, tuple):
                arrays.append(second[core])

    far_alls = [both(x) for x in far_alls]
    add(0, 0, own_sides[0], own_rest)
    add(1, 0, far_near, chips - 1)
    for s in range(1, chips):
        add(0, s, own_sides[s], s - 1)
        add(1, s, far_alls[s - 1], None)

    tables = jnp.stack([tables[0], far_table])
    height = n_row * rows_here + BLOCK
    return pl.pallas_call(
        functools.partial(front_kernel, layout, n_row, row_blocks),
        out_shape=jax.ShapeDtypeStruct((1, rows_dev, PW), F32),
        in_specs=[anywhere, anywhere] + [vmem] * (3 + len(arrays)),
        out_specs=hbm,
        scratch_shapes=[
            pltpu.VMEM((rows_dev, PW), F32),
            pltpu.VMEM((NPANEL * PW, PW), F32),
            pltpu.VMEM((2, height, PW), F32),
            pltpu.VMEM((2, height, PW), BF16),
            pltpu.SMEM(tables.shape, jnp.int32),
            pltpu.SMEM(mask.shape, jnp.int32),
            pltpu.SemaphoreType.DMA((2 + row_blocks // 3,)),
        ],
        compiler_params=params(),
        cost_estimate=cost(0),
        name="front",
    )(tables, mask, diag, *factors, *arrays)


def solution(mesh):
    in_specs = (
        P("front", None, "row", None),
        P("front", None, None, None),
        P("front", None, None),
        P("front", "row"),
    )
    out_specs = P("front", "row", "col")
    return jax.shard_map(body, mesh=mesh, in_specs=in_specs, out_specs=out_specs, check_vma=False)
```
